256 devices in a mesh: tm: 8 (over x_lo, y), freq: 32 (over x_hi, z, core).
Axes of the slice: x: 4 (x_hi: 2, x_lo: 2; x = x_hi * 2 + x_lo), y: 4, z: 8, core: 2. Of those that a mesh axis runs over, the one named last changes fastest.
Arguments:
- voltages: bfloat16 [1024, 196608], P('freq', 'tm'), may hold values from -6 to 6
- window: float32 [8, 256], replicated, may hold values from -2 to 2
Outputs:
- visibilities: float32 [2, 128, 1024, 1024], P(None, 'freq', 'tm')
The draws below stay inside these ranges and needn't reach their ends.
All inputs are finite; a program needn't handle non-finite values.
Results may differ from the reference program's by a relative error of at most 0.0031.
Values may be sent and summed in bfloat16 or wider, within the bound.
A program may use at most 128 MiB of HBM per device.

```python
import math
import jax
import jax.numpy as jnp
from jax import lax

A = 1024
P_SIZE = 256
TAPS = 8
CH = 128
SPECTRA = 768
NSAMP = 196608


def steps_of(stream_key, extent, shards, smallest, largest):
    gain, own = 1.0, jax.random.fold_in(stream_key, 6)
    for position, shards_of in shards:
        steps = jnp.exp(jax.random.uniform(jax.random.fold_in(own, position), (shards_of,), jnp.float32, smallest / len(shards), largest / len(shards)))
        gain = gain * jnp.repeat(steps, extent[position] // shards_of).reshape([-1 if axis == position else 1 for axis in range(len(extent))])
    return gain


def centred(key, extent, scale, most, pieces=(), kind=jnp.bfloat16):
    gain = steps_of(key, extent, pieces, -0.22, 0.18) if pieces else 1.0
    entries = jax.random.normal(key, extent, jnp.float32) * scale * gain
    return jnp.minimum(jnp.maximum(entries, -most), most).astype(kind)


def setup_inputs(seed: int = 0) -> dict:
    streams_of = jax.random.split(jax.random.key(seed), 3)
    voltages = centred(streams_of[0], (A, NSAMP), 1.0, 6.0, ((0, 32), (1, 8)))
    window = centred(streams_of[1], (TAPS, P_SIZE), TAPS ** -0.5, 2.0, (), jnp.float32)
    return dict(voltages=voltages, window=window)


def dft_table(length, channels):
    sample = jnp.arange(length, dtype=jnp.int32)[:, None]
    channel = jnp.arange(channels, dtype=jnp.int32)[None, :]
    phase = ((sample * channel) % length).astype(jnp.float32) * (2.0 * math.pi / length)
    return jnp.concatenate([jnp.cos(phase), -jnp.sin(phase)], axis=1) * (length ** -0.5)


def channelize(volt_block, window):
    count = volt_block.shape[0]
    frames = volt_block.astype(jnp.float32).reshape(count, SPECTRA, P_SIZE)
    padded = jnp.concatenate([jnp.zeros((count, TAPS - 1, P_SIZE), jnp.float32), frames], axis=1)
    filtered = jnp.zeros((count, SPECTRA, P_SIZE), jnp.float32)
    for tap_index in range(TAPS):
        filtered = filtered + window[tap_index][None, None, :] * padded[:, tap_index:tap_index + SPECTRA, :]
    spectra = jnp.dot(filtered.reshape(-1, P_SIZE), dft_table(P_SIZE, CH), precision=lax.Precision.HIGHEST)
    return spectra.reshape(count, SPECTRA, 2, CH).astype(jnp.bfloat16)


def channel_gram(signal):
    values = signal.astype(jnp.float32)
    paired = jnp.stack([-values[:, :, 1], values[:, :, 0]], axis=2)
    real_part = jnp.einsum("asr,bsr->ab", values, values, precision=lax.Precision.HIGHEST)
    imag_part = jnp.einsum("asr,bsr->ab", values, paired, precision=lax.Precision.HIGHEST)
    return jnp.stack([real_part, imag_part])


def reference(voltages, window):
    block_rows = 64
    grouped = voltages.reshape(A // block_rows, block_rows, NSAMP)
    spectra = lax.map(lambda rows_in: channelize(rows_in, window), grouped)
    spectra = spectra.reshape(A, SPECTRA, 2, CH)
    by_channel = jnp.moveaxis(spectra, 3, 0)
    grams = lax.map(channel_gram, by_channel)
    return jnp.transpose(grams, (1, 0, 2, 3)) * (SPECTRA ** -0.5)
```

```python
import functools
import math

import jax
import jax.numpy as jnp
from jax import lax
from jax.experimental import pallas as pl
from jax.experimental.pallas import tpu as pltpu
from jax.sharding import PartitionSpec as P

MESH = pl.DeviceIdType.MESH
LANES = 128


def from_behind(value, axis, steps):
    count = lax.axis_size(axis)
    first, last = (max(0, -steps), min(count, count - steps))
    return lax.ppermute(value, axis, [(source, source + steps) for source in range(first, last)])


def dft_table(length, channels):
    sample = jnp.arange(length, dtype=jnp.int32)[:, None]
    channel = jnp.arange(channels, dtype=jnp.int32)[None, :]
    phase = (sample * channel % length).astype(jnp.float32) * (2.0 * math.pi / length)
    return jnp.concatenate([jnp.cos(phase), -jnp.sin(phase)], axis=1) * length ** (-0.5)


def channelize(voltages, window):
    taps, period = window.shape
    channels = period // 2
    antennas = voltages.shape[0]
    blocks = voltages.reshape(antennas, -1, period)
    spec_here = blocks.shape[1]
    history = from_behind(blocks[:, spec_here - (taps - 1) :, :], "tm", 1)
    joined = jnp.concatenate([history, blocks], axis=1).astype(jnp.float32)
    filtered = jnp.zeros((antennas, spec_here, period), jnp.float32)
    for k in range(taps):
        filtered = filtered + window[k][None, None, :] * joined[:, k : k + spec_here, :]
    spectra = jnp.dot(
        filtered.reshape(-1, period), dft_table(period, channels), precision=lax.Precision.HIGHEST
    )
    return spectra.reshape(antennas, spec_here, 2, channels).astype(jnp.bfloat16)


def pack(spectra):
    antennas, spec, _, channels = spectra.shape
    main = 2 * spec // 3
    first = spectra[:, :main].transpose(3, 0, 2, 1).reshape(channels, antennas, LANES)
    rest = spectra[:, main:].reshape(2, antennas // 2, spec - main, 2, channels)
    rest = rest.transpose(4, 1, 0, 3, 2).reshape(channels, antennas // 2, LANES)
    return jnp.concatenate([first, rest], axis=1)


def correlate_kernel(
    tms, groups, scale, s_ref, r_ref, x_ref, full, swapped, outs, send1, recv1, send2, recv2, sib
):
    t, f = lax.axis_index("tm"), lax.axis_index("freq")
    g, k = f // 2, f % 2
    half = tms // 2
    peers = tms * groups
    rows = s_ref.shape[1]
    ants = 2 * rows // 3
    sibling = (t, 2 * g + 1 - k)

    barrier = pltpu.get_barrier_semaphore()

    def peer(i):
        return lax.rem(t + i // groups, tms), lax.rem(g + i % groups, groups)

    def greet(i, _):
        tt, gg = peer(i)
        pl.semaphore_signal(barrier, inc=1, device_id=(tt, 2 * gg + k), device_id_type=MESH)
        return 0

    lax.fori_loop(1, peers, greet, 0)
    pl.semaphore_signal(barrier, inc=1, device_id=sibling, device_id_type=MESH)

    def greet_source(j, _):
        tt = half * k + j

        @pl.when((tt != t) | (k != t // half))
        def _():
            pl.semaphore_signal(
                barrier, inc=1, device_id=(tt, 2 * g + t // half), device_id_type=MESH
            )

        return 0

    lax.fori_loop(0, half, greet_source, 0)
    pl.semaphore_wait(barrier, peers + half - jnp.where(k == t // half, 1, 0))

    def send_block(i, _):
        tt, gg = peer(i)
        pltpu.make_async_remote_copy(
            src_ref=s_ref.at[gg * tms + tt],
            dst_ref=x_ref.at[k, t, g],
            send_sem=send1,
            recv_sem=recv1,
            device_id=(tt, 2 * gg + k),
            device_id_type=MESH,
        ).start()
        return 0

    lax.fori_loop(1, peers, send_block, 0)
    pltpu.make_async_copy(s_ref.at[g * tms + t], x_ref.at[k, t, g], recv1).start()
    pltpu.make_async_copy(x_ref.at[k], x_ref.at[k], recv1).wait()

    share = pltpu.make_async_remote_copy(
        src_ref=x_ref.at[k],
        dst_ref=x_ref.at[k],
        send_sem=sib.at[0],
        recv_sem=sib.at[1],
        device_id=sibling,
        device_id_type=MESH,
    )
    share.start()
    share.wait_recv()

    lane = lax.broadcasted_iota(jnp.int32, (rows - ants, LANES), 1)
    low = lane < LANES // 2
    wide = tms * LANES

    def assemble(i, _):
        gg, kk = i // 2, i % 2
        base = pl.multiple_of(i * ants, ants)
        for tt in range(tms):
            full[pl.ds(base, ants), tt * LANES : (tt + 1) * LANES] = x_ref[kk, tt, gg, :ants, :]
        for tt in range(0, tms, 2):
            h0 = x_ref[kk, tt, gg, ants:, :].astype(jnp.float32)
            h1 = x_ref[kk, tt + 1, gg, ants:, :].astype(jnp.float32)
            top = jnp.where(low, h0, pltpu.roll(h1, LANES // 2, 1))
            bottom = jnp.where(low, pltpu.roll(h0, LANES // 2, 1), h1)
            at = wide + tt // 2 * LANES
            full[pl.ds(base, ants // 2), at : at + LANES] = top.astype(jnp.bfloat16)
            full[pl.ds(base + ants // 2, ants // 2), at : at + LANES] = bottom.astype(jnp.bfloat16)
        return 0

    lax.fori_loop(0, 2 * groups, assemble, 0)

    own = full.shape[0] // 2
    own_base = pl.multiple_of(k * own, own)
    step = 16
    lane = lax.broadcasted_iota(jnp.int32, (step, LANES), 1)
    low = lane < LANES // 2
    quarter = lane % (LANES // 2) < LANES // 4

    def swap(i, _):
        at = pl.multiple_of(i * step, step)
        for tile in range(full.shape[1] // LANES):
            cols = slice(tile * LANES, (tile + 1) * LANES)
            v = full[pl.ds(own_base + at, step), cols].astype(jnp.float32)
            if tile < tms:
                v = pltpu.roll(v, LANES // 2, 1)
                v = jnp.where(low, v, -v)
            else:
                v = jnp.where(
                    quarter, pltpu.roll(v, LANES - LANES // 4, 1), -pltpu.roll(v, LANES // 4, 1)
                )
            swapped[pl.ds(at, step), cols] = v.astype(jnp.bfloat16)
        return 0

    lax.fori_loop(0, own // step, swap, 0)

    tile = 256
    row_count = own // half
    slot = t % half

    def columns(n, _):
        at = pl.multiple_of(n * tile, tile)
        right = full[pl.ds(at, tile), :]
        dims = (((1,), (1,)), ((), ()))
        for part, left in enumerate((full.at[pl.ds(own_base, own), :], swapped)):
            value = lax.dot_general(
                left[...], right, dims, preferred_element_type=jnp.float32
            )
            value = (value * scale).astype(jnp.bfloat16)
            outs[:, part, :, pl.ds(at, tile)] = value.reshape(half, row_count, tile)
        for i in range(half):
            target = (half * k + i, 2 * g + t // half)
            here = (t == half * k + i) & (k == t // half)
            src = outs.at[i, :, :, pl.ds(at, tile)]
            dst = r_ref.at[:, slot, :, pl.ds(at, tile)]

            @pl.when(here)
            def _():
                pltpu.make_async_copy(src, dst, recv2).start()

            @pl.when(jnp.logical_not(here))
            def _():
                pltpu.make_async_remote_copy(
                    src_ref=src,
                    dst_ref=dst,
                    send_sem=send2,
                    recv_sem=recv2,
                    device_id=target,
                    device_id_type=MESH,
                ).start()

        return 0

    lax.fori_loop(0, full.shape[0] // tile, columns, 0)
    pltpu.make_async_copy(r_ref, r_ref, recv2).wait()

    share.wait_send()
    sent = s_ref.at[pl.ds(0, peers - 1)]
    pltpu.make_async_copy(sent, sent, send1).wait()

    @pl.when(k == t // half)
    def _():
        part = outs.at[pl.ds(0, half - 1)]
        pltpu.make_async_copy(part, part, send2).wait()

    @pl.when(k != t // half)
    def _():
        pltpu.make_async_copy(outs, outs, send2).wait()


def local(voltages, window):
    tms, freqs = lax.axis_size("tm"), lax.axis_size("freq")
    groups = freqs // 2
    half = tms // 2
    spectra = channelize(voltages, window)
    antennas, spec_here, _, channels = spectra.shape
    assert channels == tms * groups
    blocks = pack(spectra)
    rows = blocks.shape[1]
    total = antennas * freqs
    row_count = total // tms
    depth = 2 * spec_here * tms
    result = pl.pallas_call(
        functools.partial(correlate_kernel, tms, groups, (spec_here * tms) ** (-0.5)),
        out_shape=jax.ShapeDtypeStruct((2, half, row_count, total), jnp.bfloat16),
        in_specs=[pl.BlockSpec(memory_space=pltpu.VMEM)],
        out_specs=pl.BlockSpec(memory_space=pl.ANY),
        scratch_shapes=[
            pltpu.VMEM((2, tms, groups, rows, LANES), jnp.bfloat16),
            pltpu.VMEM((total, depth), jnp.bfloat16),
            pltpu.VMEM((total // 2, depth), jnp.bfloat16),
            pltpu.VMEM((half, 2, row_count, total), jnp.bfloat16),
            pltpu.SemaphoreType.DMA,
            pltpu.SemaphoreType.DMA,
            pltpu.SemaphoreType.DMA,
            pltpu.SemaphoreType.DMA,
            pltpu.SemaphoreType.DMA((2,)),
        ],
        compiler_params=pltpu.CompilerParams(
            collective_id=0, has_side_effects=True, vmem_limit_bytes=40 << 20
        ),
        cost_estimate=pl.CostEstimate(
            flops=2 * 2 * (total // 2) * total * depth, bytes_accessed=8 << 20, transcendentals=0
        ),
    )(blocks)
    return result.astype(jnp.float32)


def solution(mesh):
    return jax.shard_map(
        local,
        mesh=mesh,
        in_specs=(P("freq", "tm"), P()),
        out_specs=P(None, "freq", "tm", None),
        check_vma=False,
    )
```

```python
import functools
import math

import jax
import jax.numpy as jnp
from jax import lax
from jax.experimental import pallas as pl
from jax.experimental.pallas import tpu as pltpu
from jax.sharding import PartitionSpec as P

MESH = pl.DeviceIdType.MESH
LANES = 128
LEAD = 4


def from_behind(value, axis, steps):
    count = lax.axis_size(axis)
    first, last = (max(0, -steps), min(count, count - steps))
    return lax.ppermute(value, axis, [(source, source + steps) for source in range(first, last)])


def dft_table(length, channels):
    sample = jnp.arange(length, dtype=jnp.int32)[:, None]
    channel = jnp.arange(channels, dtype=jnp.int32)[None, :]
    phase = (sample * channel % length).astype(jnp.float32) * (2.0 * math.pi / length)
    return jnp.concatenate([jnp.cos(phase), -jnp.sin(phase)], axis=1) * length ** (-0.5)


def channelize(voltages, window):
    taps, period = window.shape
    channels = period // 2
    antennas = voltages.shape[0]
    blocks = voltages.reshape(antennas, -1, period)
    spec_here = blocks.shape[1]
    history = from_behind(blocks[:, spec_here - (taps - 1) :, :], "tm", 1)
    joined = jnp.concatenate([history, blocks], axis=1).astype(jnp.float32)
    filtered = jnp.zeros((antennas, spec_here, period), jnp.float32)
    for k in range(taps):
        filtered = filtered + window[k][None, None, :] * joined[:, k : k + spec_here, :]
    spectra = jnp.dot(
        filtered.reshape(-1, period), dft_table(period, channels), precision=lax.Precision.HIGHEST
    )
    return spectra.reshape(antennas, spec_here, 2, channels).astype(jnp.bfloat16)


def pack(spectra):
    antennas, spec, _, channels = spectra.shape
    main = 2 * spec // 3
    first = spectra[:, :main].transpose(3, 0, 2, 1).reshape(channels, antennas, LANES)
    rest = spectra[:, main:].reshape(2, antennas // 2, spec - main, 2, channels)
    rest = rest.transpose(4, 1, 0, 3, 2).reshape(channels, antennas // 2, LANES)
    return jnp.concatenate([first, rest], axis=1)


def correlate_kernel(
    tms, groups, scale, s_ref, r_ref, x_ref, right, left, outs, send1, recv1, send2, recv2, send3, recv3
):
    t, f = lax.axis_index("tm"), lax.axis_index("freq")
    g, k = f // 2, f % 2
    half = tms // 2
    peers = tms * groups
    rows = s_ref.shape[1]
    ants = 2 * rows // 3
    sibling = (t, 2 * g + 1 - k)
    mine = g // 2 % half
    first_part = lax.rem(mine + t, half)

    barrier = pltpu.get_barrier_semaphore()

    def greet(i, _):
        tt, gg = lax.rem(t + i // groups, tms), lax.rem(g + i % groups, groups)
        pl.semaphore_signal(barrier, inc=1, device_id=(tt, 2 * gg + k), device_id_type=MESH)
        return 0

    lax.fori_loop(1, peers, greet, 0)
    pl.semaphore_signal(barrier, inc=1, device_id=sibling, device_id_type=MESH)

    def greet_source(j, _):
        tt = half * k + j

        @pl.when((tt != t) | (k != t // half))
        def _():
            pl.semaphore_signal(
                barrier, inc=1, device_id=(tt, 2 * g + t // half), device_id_type=MESH
            )

        return 0

    lax.fori_loop(0, half, greet_source, 0)
    pl.semaphore_wait(barrier, peers + half - jnp.where(k == t // half, 1, 0))

    def send_phase(n):
        def send_block(i, _):
            tt = lax.rem(t + i // 4, tms)
            part = lax.rem(mine + 2 * half - tt % half - n, half)
            high = lax.rem(g // (2 * half) + i // 2 % 2, 2)
            gg = (high * half + part) * 2 + lax.rem(g + i, 2)
            src = s_ref.at[gg * tms + tt]
            dst = x_ref.at[k, mine, g // (2 * half) * 2 + g % 2, t]
            here = (tt == t) & (gg == g)

            @pl.when(here)
            def _():
                pltpu.make_async_copy(src, dst, recv1.at[n]).start()

            @pl.when(jnp.logical_not(here))
            def _():
                pltpu.make_async_remote_copy(
                    src_ref=src,
                    dst_ref=dst,
                    send_sem=send1,
                    recv_sem=recv1.at[n],
                    device_id=(tt, 2 * gg + k),
                    device_id_type=MESH,
                ).start()

            return 0

        lax.fori_loop(0, 4 * tms, send_block, 0)

    for n in range(LEAD):
        send_phase(n)

    wide = tms * LANES
    lane = lax.broadcasted_iota(jnp.int32, (16, LANES), 1)
    low = lane < LANES // 2
    quarter = lane % (LANES // 2) < LANES // 4
    block = ants * 4
    slot = t % half
    dims = (((1,), (1,)), ((), ()))

    def phase(n, _):
        part = lax.rem(first_part + n, half)
        arrived = x_ref.at[k, part]
        pltpu.make_async_copy(arrived, arrived, recv1.at[n]).wait()
        pltpu.make_async_remote_copy(
            src_ref=arrived,
            dst_ref=arrived,
            send_sem=send3,
            recv_sem=recv3.at[n],
            device_id=sibling,
            device_id_type=MESH,
        ).start()

        @pl.when(n + LEAD < half)
        def _():
            send_phase(n + LEAD)

        other = x_ref.at[1 - k, part]
        pltpu.make_async_copy(other, other, recv3.at[n]).wait()

        def assemble(i, _):
            high, kk = i // 4, i % 2
            base = pl.multiple_of(i % 4 * ants, ants)
            for tt in range(tms):
                right[part, high, pl.ds(base, ants), tt * LANES : (tt + 1) * LANES] = x_ref[
                    kk, part, i // 2, tt, :ants, :
                ]
            for tt in range(0, tms, 2):
                h0 = x_ref[kk, part, i // 2, tt, ants:, :].astype(jnp.float32)
                h1 = x_ref[kk, part, i // 2, tt + 1, ants:, :].astype(jnp.float32)
                top = jnp.where(low, h0, pltpu.roll(h1, LANES // 2, 1))
                bottom = jnp.where(low, pltpu.roll(h0, LANES // 2, 1), h1)
                at = wide + tt // 2 * LANES
                right[part, high, pl.ds(base, ants // 2), at : at + LANES] = top.astype(
                    jnp.bfloat16
                )
                right[part, high, pl.ds(base + ants // 2, ants // 2), at : at + LANES] = (
                    bottom.astype(jnp.bfloat16)
                )
            return 0

        lax.fori_loop(0, 8, assemble, 0)

        def swap(i, _):
            at = pl.multiple_of(i * 16, 16)
            for tile in range(right.shape[3] // LANES):
                cols = slice(tile * LANES, (tile + 1) * LANES)
                kept = right[part, k, pl.ds(at, 16), cols]
                left[part, 0, pl.ds(at, 16), cols] = kept
                v = kept.astype(jnp.float32)
                if tile < tms:
                    v = pltpu.roll(v, LANES // 2, 1)
                    v = jnp.where(low, v, -v)
                else:
                    v = jnp.where(
                        quarter, pltpu.roll(v, LANES - LANES // 4, 1), -pltpu.roll(v, LANES // 4, 1)
                    )
                left[part, 1, pl.ds(at, 16), cols] = v.astype(jnp.bfloat16)
            return 0

        lax.fori_loop(0, block // 16, swap, 0)

        def piece(row_part, col_part):
            value = lax.dot_general(
                left[row_part].reshape(2 * block, -1),
                right[col_part].reshape(2 * block, -1),
                dims,
                preferred_element_type=jnp.float32,
            )
            value = (value * scale).astype(jnp.bfloat16).reshape(2, block, 2 * block)
            target = half * k + row_part
            here = (t == target) & (k == t // half)
            for high in range(2):
                cols = pl.ds(pl.multiple_of((high * half + col_part) * block, block), block)
                outs[row_part, :, :, cols] = value[:, :, high * block : (high + 1) * block]
                src = outs.at[row_part, :, :, cols]
                dst = r_ref.at[:, slot, :, cols]

                @pl.when(here)
                def _():
                    pltpu.make_async_copy(src, dst, recv2).start()

                @pl.when(jnp.logical_not(here))
                def _():
                    pltpu.make_async_remote_copy(
                        src_ref=src,
                        dst_ref=dst,
                        send_sem=send2,
                        recv_sem=recv2,
                        device_id=(target, 2 * g + t // half),
                        device_id_type=MESH,
                    ).start()

        def new_piece(i, _):
            older = i // 2
            other = lax.rem(first_part + older, half)
            swap_roles = i % 2 == 1
            piece(jnp.where(swap_roles, part, other), jnp.where(swap_roles, other, part))
            return 0

        lax.fori_loop(0, 2 * n + 1, new_piece, 0)
        return 0

    lax.fori_loop(0, half, phase, 0)
    pltpu.make_async_copy(r_ref, r_ref, recv2).wait()

    pltpu.make_async_copy(x_ref.at[k], x_ref.at[k], send3).wait()
    sent = s_ref.at[pl.ds(0, peers - 1)]
    pltpu.make_async_copy(sent, sent, send1).wait()

    @pl.when(k == t // half)
    def _():
        kept = outs.at[pl.ds(0, half - 1)]
        pltpu.make_async_copy(kept, kept, send2).wait()

    @pl.when(k != t // half)
    def _():
        pltpu.make_async_copy(outs, outs, send2).wait()


def local(voltages, window):
    tms, freqs = lax.axis_size("tm"), lax.axis_size("freq")
    groups = freqs // 2
    half = tms // 2
    spectra = channelize(voltages, window)
    antennas, spec_here, _, channels = spectra.shape
    assert channels == tms * groups
    blocks = pack(spectra)
    rows = blocks.shape[1]
    total = antennas * freqs
    row_count = total // tms
    depth = 2 * spec_here * tms
    result = pl.pallas_call(
        functools.partial(correlate_kernel, tms, groups, (spec_here * tms) ** (-0.5)),
        out_shape=jax.ShapeDtypeStruct((2, half, row_count, total), jnp.bfloat16),
        in_specs=[pl.BlockSpec(memory_space=pltpu.VMEM)],
        out_specs=pl.BlockSpec(memory_space=pl.ANY),
        scratch_shapes=[
            pltpu.VMEM((2, half, groups // half, tms, rows, LANES), jnp.bfloat16),
            pltpu.VMEM((half, 2, row_count, depth), jnp.bfloat16),
            pltpu.VMEM((half, 2, row_count, depth), jnp.bfloat16),
            pltpu.VMEM((half, 2, row_count, total), jnp.bfloat16),
            pltpu.SemaphoreType.DMA,
            pltpu.SemaphoreType.DMA((half,)),
            pltpu.SemaphoreType.DMA,
            pltpu.SemaphoreType.DMA,
            pltpu.SemaphoreType.DMA,
            pltpu.SemaphoreType.DMA((half,)),
        ],
        compiler_params=pltpu.CompilerParams(
            collective_id=0, has_side_effects=True, vmem_limit_bytes=40 << 20
        ),
        cost_estimate=pl.CostEstimate(
            flops=2 * 2 * (total // 2) * total * depth, bytes_accessed=8 << 20, transcendentals=0
        ),
    )(blocks)
    return result.astype(jnp.float32)


def solution(mesh):
    return jax.shard_map(
        local,
        mesh=mesh,
        in_specs=(P("freq", "tm"), P()),
        out_specs=P(None, "freq", "tm", None),
        check_vma=False,
    )
```

```python
import functools
import math

import jax
import jax.numpy as jnp
import numpy as np
from jax import lax
from jax.experimental import pallas as pl
from jax.experimental.pallas import tpu as pltpu
from jax.sharding import PartitionSpec as P

MESH = pl.DeviceIdType.MESH
LANES = 128
LEAD = 4


def dft_table(length, channels):
    sample, channel = np.arange(length), np.arange(channels)
    phase = (channel[:, None] * sample[None, :] % length) * (2.0 * math.pi / length)
    rows = np.concatenate([np.cos(phase), -np.sin(phase)], axis=0) * length ** (-0.5)
    high = rows.astype(jnp.bfloat16)
    low = (rows - high.astype(np.float64)).astype(jnp.bfloat16)
    return np.concatenate([high, low], axis=0)


def polyphase(frames, w_ref, tile, first, groups, taps, store):
    cols = slice(tile * LANES, (tile + 1) * LANES)
    weights = [w_ref[k : k + 1, cols] for k in range(taps)]

    def group(i, held):
        held = list(held)
        for u in range(8):
            at = first + i * 8 + u
            held.append(frames(at + taps - 1, tile))
            value = weights[0] * held[0]
            for k in range(1, taps):
                value = value + weights[k] * held[k]
            held.pop(0)
            store(at, tile, value)
        return tuple(held)

    lax.fori_loop(0, groups, group, tuple(frames(first + j, tile) for j in range(taps - 1)))


def channelize(
    v_ref, w_ref, c_ref, s_ref, joined, early, late, turned, load_sem, halo_sems, t, f, tms, before
):
    taps, period = w_ref.shape
    antennas, samples = v_ref.shape
    spec = samples // period
    first, main = spec // 3, 2 * spec // 3
    tiles = period // LANES
    channels = period // 2
    halo = (taps - 1) * period
    paired = antennas // 2
    eighth = antennas // 4
    main_stride, rest_stride = main + 1, first + 1
    turn_stride = s_ref.shape[1] + 1

    def frames(j, tile):
        at = pl.multiple_of(j * period + tile * LANES, LANES)
        return joined[:, pl.ds(at, LANES)].astype(jnp.float32)

    def store_main(at, tile, value):
        for h in range(2):
            rows = pl.ds(h * paired * main_stride + at - first, paired, stride=main_stride)
            late[tile, rows, :] = value[h * paired : (h + 1) * paired]

    def store_rest(at, tile, value):
        for h in range(4):
            rows = pl.ds(h * eighth * rest_stride + at, eighth, stride=rest_stride)
            early[tile, rows, :] = value[h * eighth : (h + 1) * eighth]

    @pl.when(t == 0)
    def _():
        joined[:, :halo] = jnp.zeros((antennas, halo), jnp.bfloat16)

    own = joined.at[:, pl.ds(halo, samples)]
    pltpu.make_async_copy(v_ref, own, load_sem).wait()
    for tile in range(tiles):
        polyphase(frames, w_ref, tile, first, main // 8, taps, store_main)
    for tile in range(tiles):
        polyphase(frames, w_ref, tile, 8, first // 8 - 1, taps, store_rest)

    before()
    last = joined.at[:, pl.ds(samples, halo)]
    landing = joined.at[:, pl.ds(0, halo)]

    @pl.when(t < tms - 1)
    def _():
        pltpu.make_async_remote_copy(
            src_ref=last,
            dst_ref=landing,
            send_sem=halo_sems.at[0],
            recv_sem=halo_sems.at[1],
            device_id=(lax.rem(t + 1, tms), f),
            device_id_type=MESH,
        ).start()

    lane = lax.broadcasted_iota(jnp.int32, (channels, LANES), 1)
    low = lane < LANES // 2
    quarter = lane % (LANES // 2) < LANES // 4
    dims = (((1,), (1,)), ((), ()))

    def dft(x):
        high = x.astype(jnp.bfloat16)
        rest = (x - high.astype(jnp.float32)).astype(jnp.bfloat16)
        y = lax.dot_general(c_ref[...], high, dims, preferred_element_type=jnp.float32)
        z = lax.dot_general(
            c_ref[: 2 * channels, :], rest, dims, preferred_element_type=jnp.float32
        )
        return y[: 2 * channels] + y[2 * channels :] + z

    def gather(ref, starts, count):
        return jnp.concatenate(
            [
                jnp.concatenate([ref[tile, pl.ds(at, count), :] for at in starts], axis=0)
                for tile in range(tiles)
            ],
            axis=1,
        )

    def turn(row, value):
        turned[pl.ds(row, channels, stride=turn_stride), :] = value

    def main_part(i, _):
        starts = [(h * paired + i * 2 + p) * main_stride for p in range(2) for h in range(2)]
        y = dft(gather(late, starts, main))
        for p in range(2):
            cols = slice(p * LANES, (p + 1) * LANES)
            re, im = y[:channels, cols], y[channels:, cols]
            turn(i * 2 + p, jnp.where(low, re, pltpu.roll(im, LANES // 2, 1)))
            turn(i * 2 + p + paired, jnp.where(low, pltpu.roll(re, LANES // 2, 1), im))
        return 0

    lax.fori_loop(0, paired // 2, main_part, 0, unroll=4)

    @pl.when(t > 0)
    def _():
        pltpu.make_async_copy(landing, landing, halo_sems.at[1]).wait()

    for tile in range(tiles):
        polyphase(frames, w_ref, tile, 0, 1, taps, store_rest)

    def rest_part(i, _):
        starts = [(h * eighth + i * 2 + p) * rest_stride for p in range(2) for h in range(4)]
        y = dft(gather(early, starts, first))
        for p in range(2):
            cols = slice(p * LANES, (p + 1) * LANES)
            re, im = y[:channels, cols], y[channels:, cols]
            row = antennas + i * 2 + p
            turn(row, jnp.where(quarter, re, pltpu.roll(im, LANES // 4, 1)))
            turn(row + eighth, jnp.where(quarter, pltpu.roll(re, LANES - LANES // 4, 1), im))
        return 0

    lax.fori_loop(0, eighth // 2, rest_part, 0, unroll=4)

    def pack(i, _):
        for u in range(16):
            c = i * 16 + u
            s_ref[c] = turned[pl.ds(c * turn_stride, s_ref.shape[1]), :].astype(jnp.bfloat16)
        return 0

    lax.fori_loop(0, channels // 16, pack, 0)

    @pl.when(t < tms - 1)
    def _():
        pltpu.make_async_copy(last, last, halo_sems.at[0]).wait()


def correlate_kernel(
    tms,
    groups,
    scale,
    v_ref,
    w_ref,
    c_ref,
    r_ref,
    joined,
    early,
    late,
    turned,
    s_ref,
    x_ref,
    right,
    left,
    outs,
    load_sem,
    halo_sems,
    send1,
    recv1,
    send2,
    recv2,
    send3,
    recv3,
):
    t, f = lax.axis_index("tm"), lax.axis_index("freq")
    g, k = f // 2, f % 2
    half = tms // 2
    peers = tms * groups
    rows = s_ref.shape[1]
    ants = 2 * rows // 3
    sibling = (t, 2 * g + 1 - k)
    mine = g // 2 % half
    first_part = lax.rem(mine + t, half)

    halo = joined.shape[1] - v_ref.shape[1]
    pltpu.make_async_copy(
        v_ref, joined.at[:, pl.ds(halo, v_ref.shape[1])], load_sem
    ).start()
    barrier = pltpu.get_barrier_semaphore()

    def greet(i, _):
        tt, gg = lax.rem(t + i // groups, tms), lax.rem(g + i % groups, groups)
        pl.semaphore_signal(barrier, inc=1, device_id=(tt, 2 * gg + k), device_id_type=MESH)
        return 0

    lax.fori_loop(1, peers, greet, 0)
    pl.semaphore_signal(barrier, inc=1, device_id=sibling, device_id_type=MESH)

    def greet_source(j, _):
        tt = half * k + j

        @pl.when((tt != t) | (k != t // half))
        def _():
            pl.semaphore_signal(
                barrier, inc=1, device_id=(tt, 2 * g + t // half), device_id_type=MESH
            )

        return 0

    lax.fori_loop(0, half, greet_source, 0)

    def await_greetings():
        pl.semaphore_wait(barrier, peers + half - jnp.where(k == t // half, 1, 0))

    channelize(
        v_ref,
        w_ref,
        c_ref,
        s_ref,
        joined,
        early,
        late,
        turned,
        load_sem,
        halo_sems,
        t,
        f,
        tms,
        await_greetings,
    )

    def send_phase(n):
        def send_block(i, _):
            tt = lax.rem(t + i // 4, tms)
            part = lax.rem(mine + 2 * half - tt % half - n, half)
            high = lax.rem(g // (2 * half) + i // 2 % 2, 2)
            gg = (high * half + part) * 2 + lax.rem(g + i, 2)
            src = s_ref.at[gg * tms + tt]
            dst = x_ref.at[k, mine, g // (2 * half) * 2 + g % 2, t]
            here = (tt == t) & (gg == g)

            @pl.when(here)
            def _():
                pltpu.make_async_copy(src, dst, recv1.at[n]).start()

            @pl.when(jnp.logical_not(here))
            def _():
                pltpu.make_async_remote_copy(
                    src_ref=src,
                    dst_ref=dst,
                    send_sem=send1,
                    recv_sem=recv1.at[n],
                    device_id=(tt, 2 * gg + k),
                    device_id_type=MESH,
                ).start()

            return 0

        lax.fori_loop(0, 4 * tms, send_block, 0)

    for n in range(LEAD):
        send_phase(n)

    wide = tms * LANES
    lane = lax.broadcasted_iota(jnp.int32, (16, LANES), 1)
    low = lane < LANES // 2
    quarter = lane % (LANES // 2) < LANES // 4
    block = ants * 4
    slot = t % half
    dims = (((1,), (1,)), ((), ()))

    def phase(n, _):
        part = lax.rem(first_part + n, half)
        arrived = x_ref.at[k, part]
        pltpu.make_async_copy(arrived, arrived, recv1.at[n]).wait()
        pltpu.make_async_remote_copy(
            src_ref=arrived,
            dst_ref=arrived,
            send_sem=send3,
            recv_sem=recv3.at[n],
            device_id=sibling,
            device_id_type=MESH,
        ).start()

        @pl.when(n + LEAD < half)
        def _():
            send_phase(n + LEAD)

        other = x_ref.at[1 - k, part]
        pltpu.make_async_copy(other, other, recv3.at[n]).wait()

        def assemble(i, _):
            high, kk = i // 4, i % 2
            base = pl.multiple_of(i % 4 * ants, ants)
            for tt in range(tms):
                right[part, high, pl.ds(base, ants), tt * LANES : (tt + 1) * LANES] = x_ref[
                    kk, part, i // 2, tt, :ants, :
                ]
            for tt in range(0, tms, 2):
                h0 = x_ref[kk, part, i // 2, tt, ants:, :].astype(jnp.float32)
                h1 = x_ref[kk, part, i // 2, tt + 1, ants:, :].astype(jnp.float32)
                top = jnp.where(low, h0, pltpu.roll(h1, LANES // 2, 1))
                bottom = jnp.where(low, pltpu.roll(h0, LANES // 2, 1), h1)
                at = wide + tt // 2 * LANES
                right[part, high, pl.ds(base, ants // 2), at : at + LANES] = top.astype(
                    jnp.bfloat16
                )
                right[part, high, pl.ds(base + ants // 2, ants // 2), at : at + LANES] = (
                    bottom.astype(jnp.bfloat16)
                )
            return 0

        lax.fori_loop(0, 8, assemble, 0)

        def swap(i, _):
            at = pl.multiple_of(i * 16, 16)
            for tile in range(right.shape[3] // LANES):
                cols = slice(tile * LANES, (tile + 1) * LANES)
                kept = right[part, k, pl.ds(at, 16), cols]
                left[part, 0, pl.ds(at, 16), cols] = kept
                v = kept.astype(jnp.float32)
                if tile < tms:
                    v = pltpu.roll(v, LANES // 2, 1)
                    v = jnp.where(low, v, -v)
                else:
                    v = jnp.where(
                        quarter, pltpu.roll(v, LANES - LANES // 4, 1), -pltpu.roll(v, LANES // 4, 1)
                    )
                left[part, 1, pl.ds(at, 16), cols] = v.astype(jnp.bfloat16)
            return 0

        lax.fori_loop(0, block // 16, swap, 0)

        def piece(row_part, col_part):
            value = lax.dot_general(
                left[row_part].reshape(2 * block, -1),
                right[col_part].reshape(2 * block, -1),
                dims,
                preferred_element_type=jnp.float32,
            )
            value = (value * scale).astype(jnp.bfloat16).reshape(2, block, 2 * block)
            target = half * k + row_part
            here = (t == target) & (k == t // half)
            for high in range(2):
                cols = pl.ds(pl.multiple_of((high * half + col_part) * block, block), block)
                outs[row_part, :, :, cols] = value[:, :, high * block : (high + 1) * block]
                src = outs.at[row_part, :, :, cols]
                dst = r_ref.at[:, slot, :, cols]

                @pl.when(here)
                def _():
                    pltpu.make_async_copy(src, dst, recv2).start()

                @pl.when(jnp.logical_not(here))
                def _():
                    pltpu.make_async_remote_copy(
                        src_ref=src,
                        dst_ref=dst,
                        send_sem=send2,
                        recv_sem=recv2,
                        device_id=(target, 2 * g + t // half),
                        device_id_type=MESH,
                    ).start()

        def new_piece(i, _):
            older = i // 2
            other = lax.rem(first_part + older, half)
            swap_roles = i % 2 == 1
            piece(jnp.where(swap_roles, part, other), jnp.where(swap_roles, other, part))
            return 0

        lax.fori_loop(0, 2 * n + 1, new_piece, 0)
        return 0

    lax.fori_loop(0, half, phase, 0)
    pltpu.make_async_copy(r_ref, r_ref, recv2).wait()

    pltpu.make_async_copy(x_ref.at[k], x_ref.at[k], send3).wait()
    sent = s_ref.at[pl.ds(0, peers - 1)]
    pltpu.make_async_copy(sent, sent, send1).wait()

    @pl.when(k == t // half)
    def _():
        kept = outs.at[pl.ds(0, half - 1)]
        pltpu.make_async_copy(kept, kept, send2).wait()

    @pl.when(k != t // half)
    def _():
        pltpu.make_async_copy(outs, outs, send2).wait()


def local(voltages, window):
    tms, freqs = lax.axis_size("tm"), lax.axis_size("freq")
    groups = freqs // 2
    half = tms // 2
    taps, period = window.shape
    antennas, samples = voltages.shape
    spec_here = samples // period
    channels = period // 2
    assert channels == tms * groups
    rows = antennas * 3 // 2
    total = antennas * freqs
    row_count = total // tms
    depth = 2 * spec_here * tms
    vmem = pl.BlockSpec(memory_space=pltpu.VMEM)
    result = pl.pallas_call(
        functools.partial(correlate_kernel, tms, groups, (spec_here * tms) ** (-0.5)),
        out_shape=jax.ShapeDtypeStruct((2, half, row_count, total), jnp.bfloat16),
        in_specs=[pl.BlockSpec(memory_space=pl.ANY), vmem, vmem],
        out_specs=pl.BlockSpec(memory_space=pl.ANY),
        scratch_shapes=[
            pltpu.VMEM((antennas, samples + (taps - 1) * period), jnp.bfloat16),
            pltpu.VMEM((period // LANES, antennas * (spec_here // 3 + 1), LANES), jnp.float32),
            pltpu.VMEM((period // LANES, antennas * (2 * spec_here // 3 + 1), LANES), jnp.float32),
            pltpu.VMEM((channels * (rows + 1), LANES), jnp.float32),
            pltpu.VMEM((channels, rows, LANES), jnp.bfloat16),
            pltpu.VMEM((2, half, groups // half, tms, rows, LANES), jnp.bfloat16),
            pltpu.VMEM((half, 2, row_count, depth), jnp.bfloat16),
            pltpu.VMEM((half, 2, row_count, depth), jnp.bfloat16),
            pltpu.VMEM((half, 2, row_count, total), jnp.bfloat16),
            pltpu.SemaphoreType.DMA,
            pltpu.SemaphoreType.DMA((2,)),
            pltpu.SemaphoreType.DMA,
            pltpu.SemaphoreType.DMA((half,)),
            pltpu.SemaphoreType.DMA,
            pltpu.SemaphoreType.DMA,
            pltpu.SemaphoreType.DMA,
            pltpu.SemaphoreType.DMA((half,)),
        ],
        compiler_params=pltpu.CompilerParams(
            collective_id=0, has_side_effects=True, vmem_limit_bytes=48 << 20
        ),
        cost_estimate=pl.CostEstimate(
            flops=2 * 2 * (total // 2) * total * depth, bytes_accessed=8 << 20, transcendentals=0
        ),
    )(voltages, window, jnp.asarray(dft_table(period, channels)))
    return result.astype(jnp.float32)


def solution(mesh):
    return jax.shard_map(
        local,
        mesh=mesh,
        in_specs=(P("freq", "tm"), P()),
        out_specs=P(None, "freq", "tm", None),
        check_vma=False,
    )
```

```python
import functools
import math

import jax
import jax.numpy as jnp
import numpy as np
from jax import lax
from jax.experimental import pallas as pl
from jax.experimental.pallas import tpu as pltpu
from jax.sharding import PartitionSpec as P

MESH = pl.DeviceIdType.MESH
LANES = 128
EARLY = 2


def dft_table(length, channels):
    sample, channel = np.arange(length), np.arange(channels)
    phase = (channel[:, None] * sample[None, :] % length) * (2.0 * math.pi / length)
    rows = np.concatenate([np.cos(phase), -np.sin(phase)], axis=0) * length ** (-0.5)
    high = rows.astype(jnp.bfloat16)
    low = (rows - high.astype(np.float64)).astype(jnp.bfloat16)
    return np.concatenate([high, low], axis=0)


def polyphase(frames, w_ref, tile, first, groups, taps, store, beside=None):
    cols = slice(tile * LANES, (tile + 1) * LANES)
    weights = [w_ref[k : k + 1, cols] for k in range(taps)]

    def group(i, held):
        held = list(held)
        if beside is not None:
            beside(tile * groups + i)
        for u in range(8):
            at = first + i * 8 + u
            held.append(frames(at + taps - 1, tile))
            value = weights[0] * held[0]
            for k in range(1, taps):
                value = value + weights[k] * held[k]
            held.pop(0)
            store(at, tile, value)
        return tuple(held)

    lax.fori_loop(0, groups, group, tuple(frames(first + j, tile) for j in range(taps - 1)))


def channelize(
    v_ref, w_ref, c_ref, s_ref, joined, early, late, turned, loads, halo_sems, t, f, tms, greet, greetings,
    before, between,
):
    taps, period = w_ref.shape
    antennas, samples = v_ref.shape
    spec = samples // period
    first, main = spec // 3, 2 * spec // 3
    tiles = period // LANES
    channels = period // 2
    halo = (taps - 1) * period
    paired = antennas // 2
    eighth = antennas // 4
    main_stride, rest_stride = main + 1, first + 1
    turn_stride = s_ref.shape[1] + 1

    def frames(j, tile):
        at = pl.multiple_of(j * period + tile * LANES, LANES)
        return joined[:, pl.ds(at, LANES)].astype(jnp.float32)

    def store_main(at, tile, value):
        for h in range(2):
            rows = pl.ds(h * paired * main_stride + at - first, paired, stride=main_stride)
            late[tile, rows, :] = value[h * paired : (h + 1) * paired]

    def store_rest(at, tile, value):
        for h in range(4):
            rows = pl.ds(h * eighth * rest_stride + at, eighth, stride=rest_stride)
            early[tile, rows, :] = value[h * eighth : (h + 1) * eighth]

    @pl.when(t == 0)
    def _():
        joined[:, :halo] = jnp.zeros((antennas, halo), jnp.bfloat16)

    steps = tiles * main // 8
    each = greetings // 2 // steps
    lax.fori_loop(0, greetings - each * steps, lambda i, _: greet(i), 0)
    for load in loads:
        load.wait()
    for tile in range(tiles):
        polyphase(
            frames,
            w_ref,
            tile,
            first,
            main // 8,
            taps,
            store_main,
            lambda i: [greet(greetings - 1 - i * each - u) for u in range(each)],
        )

    lane = lax.broadcasted_iota(jnp.int32, (channels, LANES), 1)
    low = lane < LANES // 2
    quarter = lane % (LANES // 2) < LANES // 4
    dims = (((1,), (1,)), ((), ()))

    def dft(x):
        high = x.astype(jnp.bfloat16)
        rest = (x - high.astype(jnp.float32)).astype(jnp.bfloat16)
        y = lax.dot_general(c_ref[...], high, dims, preferred_element_type=jnp.float32)
        z = lax.dot_general(
            c_ref[: 2 * channels, :], rest, dims, preferred_element_type=jnp.float32
        )
        return y[: 2 * channels] + y[2 * channels :] + z

    def gather(ref, starts, count):
        return jnp.concatenate(
            [
                jnp.concatenate([ref[tile, pl.ds(at, count), :] for at in starts], axis=0)
                for tile in range(tiles)
            ],
            axis=1,
        )

    def turn(row, value):
        turned[pl.ds(row, channels, stride=turn_stride), :] = value

    def pack(at, count):
        def some(i, _):
            for u in range(16):
                c = i * 16 + u
                s_ref[c, pl.ds(at, count), :] = turned[
                    pl.ds(c * turn_stride + at, count), :
                ].astype(jnp.bfloat16)
            return 0

        lax.fori_loop(0, channels // 16, some, 0)

    def main_part(i, _):
        starts = [(h * paired + i * 2 + p) * main_stride for p in range(2) for h in range(2)]
        y = dft(gather(late, starts, main))
        for p in range(2):
            cols = slice(p * LANES, (p + 1) * LANES)
            re, im = y[:channels, cols], y[channels:, cols]
            turn(i * 2 + p, jnp.where(low, re, pltpu.roll(im, LANES // 2, 1)))
            turn(i * 2 + p + paired, jnp.where(low, pltpu.roll(re, LANES // 2, 1), im))
        return 0

    lax.fori_loop(0, paired // 2, main_part, 0, unroll=4)
    pack(0, antennas)
    for tile in range(tiles):
        polyphase(frames, w_ref, tile, 8, first // 8 - 1, taps, store_rest)

    before()
    last = joined.at[:, pl.ds(samples, halo)]
    landing = joined.at[:, pl.ds(0, halo)]

    @pl.when(t < tms - 1)
    def _():
        pltpu.make_async_remote_copy(
            src_ref=last,
            dst_ref=landing,
            send_sem=halo_sems.at[0],
            recv_sem=halo_sems.at[1],
            device_id=(lax.rem(t + 1, tms), f),
            device_id_type=MESH,
        ).start()

    between()

    @pl.when(t > 0)
    def _():
        pltpu.make_async_copy(landing, landing, halo_sems.at[1]).wait()

    for tile in range(tiles):
        polyphase(frames, w_ref, tile, 0, 1, taps, store_rest)

    def rest_part(i, _):
        starts = [(h * eighth + i * 2 + p) * rest_stride for p in range(2) for h in range(4)]
        y = dft(gather(early, starts, first))
        for p in range(2):
            cols = slice(p * LANES, (p + 1) * LANES)
            re, im = y[:channels, cols], y[channels:, cols]
            row = antennas + i * 2 + p
            turn(row, jnp.where(quarter, re, pltpu.roll(im, LANES // 4, 1)))
            turn(row + eighth, jnp.where(quarter, pltpu.roll(re, LANES - LANES // 4, 1), im))
        return 0

    lax.fori_loop(0, eighth // 2, rest_part, 0, unroll=4)
    pack(antennas, paired)

    @pl.when(t < tms - 1)
    def _():
        pltpu.make_async_copy(last, last, halo_sems.at[0]).wait()


def correlate_kernel(
    tms,
    groups,
    scale,
    v_ref,
    window_ref,
    table_ref,
    r_ref,
    joined,
    w_ref,
    c_ref,
    early,
    late,
    turned,
    s_ref,
    x_ref,
    right,
    left,
    outs,
    load_sems,
    halo_sems,
    send1,
    recv1,
    send2,
    recv2,
    send3,
    recv3,
):
    t, f = lax.axis_index("tm"), lax.axis_index("freq")
    g, k = f // 2, f % 2
    half = tms // 2
    peers = tms * groups
    rows = s_ref.shape[1]
    ants = 2 * rows // 3
    sibling = (t, 2 * g + 1 - k)
    mine = g // 2 % half
    my_high = g // (2 * half)

    halo = joined.shape[1] - v_ref.shape[1]
    loads = [
        pltpu.make_async_copy(source, target, load_sems.at[i])
        for i, (source, target) in enumerate(
            (
                (v_ref, joined.at[:, pl.ds(halo, v_ref.shape[1])]),
                (window_ref, w_ref),
                (table_ref, c_ref),
            )
        )
    ]
    for load in loads:
        load.start()
    barrier = pltpu.get_barrier_semaphore()

    def greet(n):
        tt, gg = lax.rem(t + n // groups, tms), lax.rem(g + n % groups, groups)
        to = jnp.where(n == 0, 2 * g + 1 - k, 2 * gg + k)
        pl.semaphore_signal(barrier, inc=1, device_id=(tt, to), device_id_type=MESH)
        return 0

    for j in range(half):
        pl.semaphore_signal(
            barrier, inc=1, device_id=(half * k + j, 2 * g + 1 - k), device_id_type=MESH
        )

    def await_greetings():
        pl.semaphore_wait(barrier, peers + jnp.where(k == t // half, 0, tms))

    def send_phase(n, first_row, row_count):
        def send_block(i, _):
            tt = lax.rem(t + i // 2, tms)
            part = lax.rem(mine + 2 * half - tt % half - n // 2, half)
            high = lax.rem(my_high + tt // half + n % 2, 2)
            gg = (high * half + part) * 2 + lax.rem(g + i, 2)
            some = pl.ds(first_row, row_count)
            src = s_ref.at[gg * tms + tt, some]
            dst = x_ref.at[k, mine, my_high, g % 2, t, some]
            here = (tt == t) & (gg == g)

            @pl.when(here)
            def _():
                pltpu.make_async_copy(src, dst, recv1.at[n]).start()

            @pl.when(jnp.logical_not(here))
            def _():
                pltpu.make_async_remote_copy(
                    src_ref=src,
                    dst_ref=dst,
                    send_sem=send1,
                    recv_sem=recv1.at[n],
                    device_id=(tt, 2 * gg + k),
                    device_id_type=MESH,
                ).start()

            return 0

        lax.fori_loop(0, 2 * tms, send_block, 0)
        return 0

    def send_phases(first, last, first_row, row_count):
        lax.fori_loop(first, last, lambda n, _: send_phase(n, first_row, row_count), 0)

    channelize(
        v_ref,
        w_ref,
        c_ref,
        s_ref,
        joined,
        early,
        late,
        turned,
        loads,
        halo_sems,
        t,
        f,
        tms,
        greet,
        peers,
        await_greetings,
        lambda: send_phases(0, EARLY, 0, ants),
    )
    send_phases(0, EARLY, ants, rows - ants)
    send_phases(EARLY, tms, 0, rows)

    wide = tms * LANES
    lane = lax.broadcasted_iota(jnp.int32, (16, LANES), 1)
    low = lane < LANES // 2
    quarter = lane % (LANES // 2) < LANES // 4
    block = ants * 4
    own = block // 2
    slot = t % half
    dims = (((1,), (1,)), ((), ()))

    def place(n):
        return lax.rem(my_high + t // half + n % 2, 2), lax.rem(mine + t + n // 2, half)

    def phase(n, _):
        high, part = place(n)
        arrived = x_ref.at[k, part, high]
        pltpu.make_async_copy(arrived, arrived, recv1.at[n]).wait()
        pltpu.make_async_remote_copy(
            src_ref=arrived,
            dst_ref=arrived,
            send_sem=send3,
            recv_sem=recv3.at[n],
            device_id=sibling,
            device_id_type=MESH,
        ).start()
        other = x_ref.at[1 - k, part, high]
        pltpu.make_async_copy(other, other, recv3.at[n]).wait()

        def assemble(i, _):
            kk, low_g = i % 2, i // 2
            base = pl.multiple_of(i * ants, ants)
            for tt in range(tms):
                right[n, pl.ds(base, ants), tt * LANES : (tt + 1) * LANES] = x_ref[
                    kk, part, high, low_g, tt, :ants, :
                ]
            for tt in range(0, tms, 2):
                h0 = x_ref[kk, part, high, low_g, tt, ants:, :].astype(jnp.float32)
                h1 = x_ref[kk, part, high, low_g, tt + 1, ants:, :].astype(jnp.float32)
                top = jnp.where(low, h0, pltpu.roll(h1, LANES // 2, 1))
                bottom = jnp.where(low, pltpu.roll(h0, LANES // 2, 1), h1)
                cols = slice(wide + tt // 2 * LANES, wide + (tt // 2 + 1) * LANES)
                right[n, pl.ds(base, ants // 2), cols] = top.astype(jnp.bfloat16)
                right[n, pl.ds(base + ants // 2, ants // 2), cols] = bottom.astype(jnp.bfloat16)
            return 0

        lax.fori_loop(0, 4, assemble, 0)

        def swap(i, _):
            at = pl.multiple_of(i * 16, 16)
            for tile in range(right.shape[2] // LANES):
                cols = slice(tile * LANES, (tile + 1) * LANES)
                kept = right[n, pl.ds(pl.multiple_of(k * own + at, 16), 16), cols]
                left[n, 0, pl.ds(at, 16), cols] = kept
                v = kept.astype(jnp.float32)
                if tile < tms:
                    v = pltpu.roll(v, LANES // 2, 1)
                    v = jnp.where(low, v, -v)
                else:
                    v = jnp.where(
                        quarter, pltpu.roll(v, LANES - LANES // 4, 1), -pltpu.roll(v, LANES // 4, 1)
                    )
                left[n, 1, pl.ds(at, 16), cols] = v.astype(jnp.bfloat16)
            return 0

        lax.fori_loop(0, own // 16, swap, 0)

        def piece(row, row_count, col, col_count):
            value = lax.dot_general(
                left[pl.ds(row, row_count)].reshape(row_count * block, -1),
                right[pl.ds(col, col_count)].reshape(col_count * block, -1),
                dims,
                preferred_element_type=jnp.float32,
            )
            value = (value * scale).astype(jnp.bfloat16)
            value = value.reshape(row_count, 2, own, col_count * block)
            for r in range(row_count):
                to_high, to_part = place(row + r)
                target = to_high * half + to_part
                here = (t == target) & (k == t // half)
                for c in range(col_count):
                    at_high, at_part = place(col + c)
                    cols = pl.ds(pl.multiple_of((at_high * half + at_part) * block, block), block)
                    outs[row + r, :, :, cols] = value[r, :, :, c * block : (c + 1) * block]
                    src = outs.at[row + r, :, :, cols]
                    dst = r_ref.at[:, slot, pl.ds(pl.multiple_of(k * own, own), own), cols]

                    @pl.when(here)
                    def _():
                        pltpu.make_async_copy(src, dst, recv2).start()

                    @pl.when(jnp.logical_not(here))
                    def _():
                        pltpu.make_async_remote_copy(
                            src_ref=src,
                            dst_ref=dst,
                            send_sem=send2,
                            recv_sem=recv2,
                            device_id=(target, 2 * g + t // half),
                            device_id_type=MESH,
                        ).start()

        def row_pair(i, _):
            piece(n, 1, 2 * i, 2)
            return 0

        def column_pair(i, _):
            piece(2 * i, 2, n, 1)
            return 0

        lax.fori_loop(0, (n + 1) // 2, row_pair, 0)
        lax.fori_loop(0, n // 2, column_pair, 0)
        piece(n - n % 2, 1, n, 1)
        return 0

    lax.fori_loop(0, tms, phase, 0)
    pltpu.make_async_copy(r_ref, r_ref, recv2).wait()

    pltpu.make_async_copy(x_ref.at[k], x_ref.at[k], send3).wait()
    sent = s_ref.at[pl.ds(0, peers - 1)]
    pltpu.make_async_copy(sent, sent, send1).wait()

    @pl.when(k == t // half)
    def _():
        kept = outs.at[pl.ds(0, tms - 1)]
        pltpu.make_async_copy(kept, kept, send2).wait()

    @pl.when(k != t // half)
    def _():
        pltpu.make_async_copy(outs, outs, send2).wait()


def local(voltages, window):
    tms, freqs = lax.axis_size("tm"), lax.axis_size("freq")
    groups = freqs // 2
    half = tms // 2
    taps, period = window.shape
    antennas, samples = voltages.shape
    spec_here = samples // period
    channels = period // 2
    assert channels == tms * groups
    rows = antennas * 3 // 2
    total = antennas * freqs
    row_count = total // tms
    depth = 2 * spec_here * tms
    result = pl.pallas_call(
        functools.partial(correlate_kernel, tms, groups, (spec_here * tms) ** (-0.5)),
        out_shape=jax.ShapeDtypeStruct((2, half, row_count, total), jnp.bfloat16),
        in_specs=[pl.BlockSpec(memory_space=pl.ANY)] * 3,
        out_specs=pl.BlockSpec(memory_space=pl.ANY),
        scratch_shapes=[
            pltpu.VMEM((antennas, samples + (taps - 1) * period), jnp.bfloat16),
            pltpu.VMEM(window.shape, jnp.float32),
            pltpu.VMEM((4 * channels, period), jnp.bfloat16),
            pltpu.VMEM((period // LANES, antennas * (spec_here // 3 + 1), LANES), jnp.float32),
            pltpu.VMEM((period // LANES, antennas * (2 * spec_here // 3 + 1), LANES), jnp.float32),
            pltpu.VMEM((channels * (rows + 1), LANES), jnp.float32),
            pltpu.VMEM((channels, rows, LANES), jnp.bfloat16),
            pltpu.VMEM((2, half, 2, 2, tms, rows, LANES), jnp.bfloat16),
            pltpu.VMEM((tms, row_count, depth), jnp.bfloat16),
            pltpu.VMEM((tms, 2, row_count // 2, depth), jnp.bfloat16),
            pltpu.VMEM((tms, 2, row_count // 2, total), jnp.bfloat16),
            pltpu.SemaphoreType.DMA((3,)),
            pltpu.SemaphoreType.DMA((2,)),
            pltpu.SemaphoreType.DMA,
            pltpu.SemaphoreType.DMA((tms,)),
            pltpu.SemaphoreType.DMA,
            pltpu.SemaphoreType.DMA,
            pltpu.SemaphoreType.DMA,
            pltpu.SemaphoreType.DMA((tms,)),
        ],
        compiler_params=pltpu.CompilerParams(
            collective_id=0, has_side_effects=True, vmem_limit_bytes=60 << 20
        ),
        cost_estimate=pl.CostEstimate(
            flops=2 * 2 * (total // 2) * total * depth, bytes_accessed=8 << 20, transcendentals=0
        ),
    )(voltages, window, jnp.asarray(dft_table(period, channels)))
    return result.astype(jnp.float32)


def solution(mesh):
    return jax.shard_map(
        local,
        mesh=mesh,
        in_specs=(P("freq", "tm"), P()),
        out_specs=P(None, "freq", "tm", None),
        check_vma=False,
    )
```

```python
import functools
import math

import jax
import jax.numpy as jnp
import numpy as np
from jax import lax
from jax.experimental import pallas as pl
from jax.experimental.pallas import tpu as pltpu
from jax.sharding import PartitionSpec as P

MESH = pl.DeviceIdType.MESH
LANES = 128
EARLY = 2


def dft_table(length, channels):
    sample, channel = np.arange(length), np.arange(channels)
    phase = (channel[:, None] * sample[None, :] % length) * (2.0 * math.pi / length)
    rows = np.concatenate([np.cos(phase), -np.sin(phase)], axis=0) * length ** (-0.5)
    high = rows.astype(jnp.bfloat16)
    low = (rows - high.astype(np.float64)).astype(jnp.bfloat16)
    return np.concatenate([high, low], axis=0)


def polyphase(frames, w_ref, tile, first, groups, taps, store, beside=None):
    cols = slice(tile * LANES, (tile + 1) * LANES)
    weights = [w_ref[k : k + 1, cols] for k in range(taps)]

    def group(i, held):
        held = list(held)
        if beside is not None:
            beside(tile * groups + i)
        for u in range(8):
            at = first + i * 8 + u
            held.append(frames(at + taps - 1, tile))
            value = weights[0] * held[0]
            for k in range(1, taps):
                value = value + weights[k] * held[k]
            held.pop(0)
            store(at, tile, value)
        return tuple(held)

    lax.fori_loop(0, groups, group, tuple(frames(first + j, tile) for j in range(taps - 1)))


def channelize(
    v_ref, w_ref, c_ref, s_ref, joined, early, late, turned, loads, halo_sems, t, f, tms, greet, greetings,
    before, between,
):
    taps, period = w_ref.shape
    antennas, samples = v_ref.shape
    spec = samples // period
    first, main = spec // 3, 2 * spec // 3
    tiles = period // LANES
    channels = period // 2
    halo = (taps - 1) * period
    paired = antennas // 2
    eighth = antennas // 4
    main_stride, rest_stride = main + 1, first + 1
    turn_stride = s_ref.shape[1] + 1

    def frames(j, tile):
        at = pl.multiple_of(j * period + tile * LANES, LANES)
        return joined[:, pl.ds(at, LANES)].astype(jnp.float32)

    def store_main(at, tile, value):
        for h in range(2):
            rows = pl.ds(h * paired * main_stride + at - first, paired, stride=main_stride)
            late[tile, rows, :] = value[h * paired : (h + 1) * paired]

    def store_rest(at, tile, value):
        for h in range(4):
            rows = pl.ds(h * eighth * rest_stride + at, eighth, stride=rest_stride)
            early[tile, rows, :] = value[h * eighth : (h + 1) * eighth]

    @pl.when(t == 0)
    def _():
        joined[:, :halo] = jnp.zeros((antennas, halo), jnp.bfloat16)

    steps = tiles * main // 8
    each = greetings // 2 // steps
    lax.fori_loop(0, greetings - each * steps, lambda i, _: greet(i), 0)
    for load in loads:
        load.wait()
    for tile in range(tiles):
        polyphase(
            frames,
            w_ref,
            tile,
            first,
            main // 8,
            taps,
            store_main,
            lambda i: [greet(greetings - 1 - i * each - u) for u in range(each)],
        )

    lane = lax.broadcasted_iota(jnp.int32, (channels, LANES), 1)
    low = lane < LANES // 2
    quarter = lane % (LANES // 2) < LANES // 4
    dims = (((1,), (1,)), ((), ()))

    def dft(x):
        high = x.astype(jnp.bfloat16)
        rest = (x - high.astype(jnp.float32)).astype(jnp.bfloat16)
        y = lax.dot_general(c_ref[...], high, dims, preferred_element_type=jnp.float32)
        z = lax.dot_general(
            c_ref[: 2 * channels, :], rest, dims, preferred_element_type=jnp.float32
        )
        return y[: 2 * channels] + y[2 * channels :] + z

    def gather(ref, starts, count):
        return jnp.concatenate(
            [
                jnp.concatenate([ref[tile, pl.ds(at, count), :] for at in starts], axis=0)
                for tile in range(tiles)
            ],
            axis=1,
        )

    def turn(row, value):
        turned[pl.ds(row, channels, stride=turn_stride), :] = value

    def pack(at, count):
        def some(i, _):
            for u in range(16):
                c = i * 16 + u
                s_ref[c, pl.ds(at, count), :] = turned[
                    pl.ds(c * turn_stride + at, count), :
                ].astype(jnp.bfloat16)
            return 0

        lax.fori_loop(0, channels // 16, some, 0)

    def main_part(i, _):
        starts = [(h * paired + i * 2 + p) * main_stride for p in range(2) for h in range(2)]
        y = dft(gather(late, starts, main))
        for p in range(2):
            cols = slice(p * LANES, (p + 1) * LANES)
            re, im = y[:channels, cols], y[channels:, cols]
            turn(i * 2 + p, jnp.where(low, re, pltpu.roll(im, LANES // 2, 1)))
            turn(i * 2 + p + paired, jnp.where(low, pltpu.roll(re, LANES // 2, 1), im))
        return 0

    lax.fori_loop(0, paired // 2, main_part, 0, unroll=4)
    pack(0, antennas)
    for tile in range(tiles):
        polyphase(frames, w_ref, tile, 8, first // 8 - 1, taps, store_rest)

    before()
    last = joined.at[:, pl.ds(samples, halo)]
    landing = joined.at[:, pl.ds(0, halo)]

    @pl.when(t < tms - 1)
    def _():
        pltpu.make_async_remote_copy(
            src_ref=last,
            dst_ref=landing,
            send_sem=halo_sems.at[0],
            recv_sem=halo_sems.at[1],
            device_id=(lax.rem(t + 1, tms), f),
            device_id_type=MESH,
        ).start()

    between()

    @pl.when(t > 0)
    def _():
        pltpu.make_async_copy(landing, landing, halo_sems.at[1]).wait()

    for tile in range(tiles):
        polyphase(frames, w_ref, tile, 0, 1, taps, store_rest)

    def rest_part(i, _):
        starts = [(h * eighth + i * 2 + p) * rest_stride for p in range(2) for h in range(4)]
        y = dft(gather(early, starts, first))
        for p in range(2):
            cols = slice(p * LANES, (p + 1) * LANES)
            re, im = y[:channels, cols], y[channels:, cols]
            row = antennas + i * 2 + p
            turn(row, jnp.where(quarter, re, pltpu.roll(im, LANES // 4, 1)))
            turn(row + eighth, jnp.where(quarter, pltpu.roll(re, LANES - LANES // 4, 1), im))
        return 0

    lax.fori_loop(0, eighth // 2, rest_part, 0, unroll=4)
    pack(antennas, paired)

    @pl.when(t < tms - 1)
    def _():
        pltpu.make_async_copy(last, last, halo_sems.at[0]).wait()


def correlate_kernel(
    tms,
    groups,
    scale,
    v_ref,
    window_ref,
    table_ref,
    r_ref,
    joined,
    w_ref,
    c_ref,
    early,
    late,
    turned,
    s_ref,
    x_ref,
    right,
    left,
    outs,
    load_sems,
    halo_sems,
    send1,
    recv1,
    send2,
    recv2,
    send3,
    recv3,
):
    t, f = lax.axis_index("tm"), lax.axis_index("freq")
    g, k = f // 2, f % 2
    half = tms // 2
    peers = tms * groups
    rows = s_ref.shape[1]
    ants = 2 * rows // 3
    sibling = (t, 2 * g + 1 - k)
    mine = g // 2 % half
    my_high = g // (2 * half)

    halo = joined.shape[1] - v_ref.shape[1]
    loads = [
        pltpu.make_async_copy(source, target, load_sems.at[i])
        for i, (source, target) in enumerate(
            (
                (v_ref, joined.at[:, pl.ds(halo, v_ref.shape[1])]),
                (window_ref, w_ref),
                (table_ref, c_ref),
            )
        )
    ]
    for load in loads:
        load.start()
    barrier = pltpu.get_barrier_semaphore()

    def greet(n):
        tt, gg = lax.rem(t + n // groups, tms), lax.rem(g + n % groups, groups)
        to = jnp.where(n == 0, 2 * g + 1 - k, 2 * gg + k)
        pl.semaphore_signal(barrier, inc=1, device_id=(tt, to), device_id_type=MESH)
        return 0

    for j in range(half):
        pl.semaphore_signal(
            barrier, inc=1, device_id=(half * k + j, 2 * g + 1 - k), device_id_type=MESH
        )

    def await_greetings():
        pl.semaphore_wait(barrier, peers + jnp.where(k == t // half, 0, tms))

    def send_phase(n, first_row, row_count):
        def send_block(i, _):
            tt = lax.rem(t + i // 2, tms)
            part = lax.rem(mine + 2 * half - tt % half - n // 2, half)
            high = lax.rem(my_high + tt // half + n % 2, 2)
            gg = (high * half + part) * 2 + lax.rem(g + i, 2)
            some = pl.ds(first_row, row_count)
            src = s_ref.at[gg * tms + tt, some]
            dst = x_ref.at[k, mine, my_high, g % 2, t, some]
            here = (tt == t) & (gg == g)

            @pl.when(here)
            def _():
                pltpu.make_async_copy(src, dst, recv1.at[n]).start()

            @pl.when(jnp.logical_not(here))
            def _():
                pltpu.make_async_remote_copy(
                    src_ref=src,
                    dst_ref=dst,
                    send_sem=send1,
                    recv_sem=recv1.at[n],
                    device_id=(tt, 2 * gg + k),
                    device_id_type=MESH,
                ).start()

            return 0

        lax.fori_loop(0, 2 * tms, send_block, 0)
        return 0

    def send_phases(first, last, first_row, row_count):
        lax.fori_loop(first, last, lambda n, _: send_phase(n, first_row, row_count), 0)

    channelize(
        v_ref,
        w_ref,
        c_ref,
        s_ref,
        joined,
        early,
        late,
        turned,
        loads,
        halo_sems,
        t,
        f,
        tms,
        greet,
        peers,
        await_greetings,
        lambda: send_phases(0, EARLY, 0, ants),
    )
    send_phases(0, EARLY, ants, rows - ants)
    send_phases(EARLY, tms, 0, rows)

    wide = tms * LANES
    lane = lax.broadcasted_iota(jnp.int32, (ants, LANES), 1)
    low = lane < LANES // 2
    quarter = lane % (LANES // 2) < LANES // 4
    block = ants * 4
    own = block // 2
    slot = t % half
    dims = (((1,), (1,)), ((), ()))

    def place(n):
        return lax.rem(my_high + t // half + n % 2, 2), lax.rem(mine + t + n // 2, half)

    def phase(n, _):
        high, part = place(n)
        arrived = x_ref.at[k, part, high]
        pltpu.make_async_copy(arrived, arrived, recv1.at[n]).wait()
        pltpu.make_async_remote_copy(
            src_ref=arrived,
            dst_ref=arrived,
            send_sem=send3,
            recv_sem=recv3.at[n],
            device_id=sibling,
            device_id_type=MESH,
        ).start()

        def assemble(kk, mine_too):
            for low_g in range(2):
                base = pl.multiple_of((2 * low_g + kk) * ants, ants)

                def put(at, cols, value, turned_value):
                    count = value.shape[0]
                    right[n, pl.ds(base + at, count), cols] = value
                    if mine_too:
                        left[n, 0, low_g * ants + at : low_g * ants + at + count, cols] = value
                        left[n, 1, low_g * ants + at : low_g * ants + at + count, cols] = (
                            turned_value(value)
                        )

                def turn_wide(v):
                    v = pltpu.roll(v, LANES // 2, 1)
                    return jnp.where(low[: v.shape[0]], v, -v)

                def turn_narrow(v):
                    ahead = pltpu.roll(v, LANES - LANES // 4, 1)
                    behind = pltpu.roll(v, LANES // 4, 1)
                    return jnp.where(quarter[: v.shape[0]], ahead, -behind)

                for tt in range(tms):
                    cols = slice(tt * LANES, (tt + 1) * LANES)
                    put(0, cols, x_ref[kk, part, high, low_g, tt, :ants, :], turn_wide)
                for tt in range(0, tms, 2):
                    h0 = x_ref[kk, part, high, low_g, tt, ants:, :]
                    h1 = x_ref[kk, part, high, low_g, tt + 1, ants:, :]
                    some = low[: ants // 2]
                    cols = slice(wide + tt // 2 * LANES, wide + (tt // 2 + 1) * LANES)
                    top = jnp.where(some, h0, pltpu.roll(h1, LANES // 2, 1))
                    put(0, cols, top, turn_narrow)
                    bottom = jnp.where(some, pltpu.roll(h0, LANES // 2, 1), h1)
                    put(ants // 2, cols, bottom, turn_narrow)

        assemble(k, True)

        def piece(row, row_count, col, col_count):
            value = lax.dot_general(
                left[pl.ds(row, row_count)].reshape(row_count * block, -1),
                right[pl.ds(col, col_count)].reshape(col_count * block, -1),
                dims,
                preferred_element_type=jnp.float32,
            )
            value = (value * scale).astype(jnp.bfloat16)
            value = value.reshape(row_count, 2, 2, ants, col_count * block)
            for r in range(row_count):
                to_high, to_part = place(row + r)
                target = to_high * half + to_part
                here = (t == target) & (k == t // half)
                for c in range(col_count):
                    at_high, at_part = place(col + c)
                    cols = pl.ds(pl.multiple_of((at_high * half + at_part) * block, block), block)
                    outs[row + r, :, :, :, cols] = value[r, :, :, :, c * block : (c + 1) * block]
                    src = outs.at[row + r, :, :, :, cols]
                    dst = r_ref.at[:, slot, :, k, :, cols]

                    @pl.when(here)
                    def _():
                        pltpu.make_async_copy(src, dst, recv2).start()

                    @pl.when(jnp.logical_not(here))
                    def _():
                        pltpu.make_async_remote_copy(
                            src_ref=src,
                            dst_ref=dst,
                            send_sem=send2,
                            recv_sem=recv2,
                            device_id=(target, 2 * g + t // half),
                            device_id_type=MESH,
                        ).start()

        def row_pair(i, _):
            piece(n, 1, 2 * i, 2)
            return 0

        def column_pair(i, _):
            piece(2 * i, 2, n, 1)
            return 0

        lax.fori_loop(0, n // 2, row_pair, 0)

        @pl.when(n % 2 == 1)
        def _():
            piece(n, 1, n - 1, 1)

        other = x_ref.at[1 - k, part, high]
        pltpu.make_async_copy(other, other, recv3.at[n]).wait()
        assemble(1 - k, False)
        lax.fori_loop(0, (n + 1) // 2, column_pair, 0)

        @pl.when(n % 2 == 0)
        def _():
            piece(n, 1, n, 1)

        return 0

    lax.fori_loop(0, tms, phase, 0)
    pltpu.make_async_copy(r_ref, r_ref, recv2).wait()

    pltpu.make_async_copy(x_ref.at[k], x_ref.at[k], send3).wait()
    sent = s_ref.at[pl.ds(0, peers - 1)]
    pltpu.make_async_copy(sent, sent, send1).wait()

    @pl.when(k == t // half)
    def _():
        kept = outs.at[pl.ds(0, tms - 1)]
        pltpu.make_async_copy(kept, kept, send2).wait()

    @pl.when(k != t // half)
    def _():
        pltpu.make_async_copy(outs, outs, send2).wait()


def local(voltages, window):
    tms, freqs = lax.axis_size("tm"), lax.axis_size("freq")
    groups = freqs // 2
    half = tms // 2
    taps, period = window.shape
    antennas, samples = voltages.shape
    spec_here = samples // period
    channels = period // 2
    assert channels == tms * groups
    rows = antennas * 3 // 2
    total = antennas * freqs
    row_count = total // tms
    depth = 2 * spec_here * tms
    result = pl.pallas_call(
        functools.partial(correlate_kernel, tms, groups, (spec_here * tms) ** (-0.5)),
        out_shape=jax.ShapeDtypeStruct((2, half, 2, 2, antennas, total), jnp.bfloat16),
        in_specs=[pl.BlockSpec(memory_space=pl.ANY)] * 3,
        out_specs=pl.BlockSpec(memory_space=pl.ANY),
        scratch_shapes=[
            pltpu.VMEM((antennas, samples + (taps - 1) * period), jnp.bfloat16),
            pltpu.VMEM(window.shape, jnp.float32),
            pltpu.VMEM((4 * channels, period), jnp.bfloat16),
            pltpu.VMEM((period // LANES, antennas * (spec_here // 3 + 1), LANES), jnp.float32),
            pltpu.VMEM((period // LANES, antennas * (2 * spec_here // 3 + 1), LANES), jnp.float32),
            pltpu.VMEM((channels * (rows + 1), LANES), jnp.float32),
            pltpu.VMEM((channels, rows, LANES), jnp.bfloat16),
            pltpu.VMEM((2, half, 2, 2, tms, rows, LANES), jnp.bfloat16),
            pltpu.VMEM((tms, row_count, depth), jnp.bfloat16),
            pltpu.VMEM((tms, 2, row_count // 2, depth), jnp.bfloat16),
            pltpu.VMEM((tms, 2, 2, antennas, total), jnp.bfloat16),
            pltpu.SemaphoreType.DMA((3,)),
            pltpu.SemaphoreType.DMA((2,)),
            pltpu.SemaphoreType.DMA,
            pltpu.SemaphoreType.DMA((tms,)),
            pltpu.SemaphoreType.DMA,
            pltpu.SemaphoreType.DMA,
            pltpu.SemaphoreType.DMA,
            pltpu.SemaphoreType.DMA((tms,)),
        ],
        compiler_params=pltpu.CompilerParams(
            collective_id=0, has_side_effects=True, vmem_limit_bytes=60 << 20
        ),
        cost_estimate=pl.CostEstimate(
            flops=2 * 2 * (total // 2) * total * depth, bytes_accessed=8 << 20, transcendentals=0
        ),
    )(voltages, window, jnp.asarray(dft_table(period, channels)))
    return result.reshape(2, half, row_count, total).astype(jnp.float32)


def solution(mesh):
    return jax.shard_map(
        local,
        mesh=mesh,
        in_specs=(P("freq", "tm"), P()),
        out_specs=P(None, "freq", "tm", None),
        check_vma=False,
    )
```

```python
import functools
import math

import jax
import jax.numpy as jnp
import numpy as np
from jax import lax
from jax.experimental import pallas as pl
from jax.experimental.pallas import tpu as pltpu
from jax.sharding import PartitionSpec as P

MESH = pl.DeviceIdType.MESH
LANES = 128
EARLY = 2


def dft_table(length, channels):
    sample, channel = np.arange(length), np.arange(channels)
    phase = (channel[:, None] * sample[None, :] % length) * (2.0 * math.pi / length)
    rows = np.concatenate([np.cos(phase), -np.sin(phase)], axis=0) * length ** (-0.5)
    high = rows.astype(jnp.bfloat16)
    low = (rows - high.astype(np.float64)).astype(jnp.bfloat16)
    return np.concatenate([high, low], axis=0)


def polyphase(frames, w_ref, tile, first, groups, taps, store, beside=None):
    cols = slice(tile * LANES, (tile + 1) * LANES)
    weights = [w_ref[k : k + 1, cols] for k in range(taps)]

    def group(i, held):
        held = list(held)
        if beside is not None:
            beside(tile * groups + i)
        for u in range(8):
            at = first + i * 8 + u
            held.append(frames(at + taps - 1, tile))
            value = weights[0] * held[0]
            for k in range(1, taps):
                value = value + weights[k] * held[k]
            held.pop(0)
            store(at, tile, value)
        return tuple(held)

    lax.fori_loop(0, groups, group, tuple(frames(first + j, tile) for j in range(taps - 1)))


def channelize(
    v_ref, w_ref, c_ref, s_ref, joined, early, late, turned, loads, halo_sems, t, f, tms, greet, greetings,
    before, between,
):
    taps, period = w_ref.shape
    antennas, samples = v_ref.shape
    spec = samples // period
    first, main = spec // 3, 2 * spec // 3
    tiles = period // LANES
    channels = period // 2
    halo = (taps - 1) * period
    paired = antennas // 2
    eighth = antennas // 4
    main_stride, rest_stride = main + 1, first + 1
    turn_stride = s_ref.shape[1] + 1

    def frames(j, tile):
        at = pl.multiple_of(j * period + tile * LANES, LANES)
        return joined[:, pl.ds(at, LANES)].astype(jnp.float32)

    def store_main(at, tile, value):
        for h in range(2):
            rows = pl.ds(h * paired * main_stride + at - first, paired, stride=main_stride)
            late[tile, rows, :] = value[h * paired : (h + 1) * paired]

    def store_rest(at, tile, value):
        for h in range(4):
            rows = pl.ds(h * eighth * rest_stride + at, eighth, stride=rest_stride)
            early[tile, rows, :] = value[h * eighth : (h + 1) * eighth]

    @pl.when(t == 0)
    def _():
        joined[:, :halo] = jnp.zeros((antennas, halo), jnp.bfloat16)

    steps = tiles * main // 8
    each = greetings // 2 // steps
    lax.fori_loop(0, greetings - each * steps, lambda i, _: greet(i), 0)
    for load in loads:
        load.wait()
    for tile in range(tiles):
        polyphase(
            frames,
            w_ref,
            tile,
            first,
            main // 8,
            taps,
            store_main,
            lambda i: [greet(greetings - 1 - i * each - u) for u in range(each)],
        )

    lane = lax.broadcasted_iota(jnp.int32, (channels, LANES), 1)
    low = lane < LANES // 2
    quarter = lane % (LANES // 2) < LANES // 4
    dims = (((1,), (1,)), ((), ()))

    def dft(x):
        high = x.astype(jnp.bfloat16)
        rest = (x - high.astype(jnp.float32)).astype(jnp.bfloat16)
        y = lax.dot_general(c_ref[...], high, dims, preferred_element_type=jnp.float32)
        z = lax.dot_general(
            c_ref[: 2 * channels, :], rest, dims, preferred_element_type=jnp.float32
        )
        return y[: 2 * channels] + y[2 * channels :] + z

    def gather(ref, starts, count):
        return jnp.concatenate(
            [
                jnp.concatenate([ref[tile, pl.ds(at, count), :] for at in starts], axis=0)
                for tile in range(tiles)
            ],
            axis=1,
        )

    def turn(row, value):
        turned[pl.ds(row, channels, stride=turn_stride), :] = value

    def pack(at, count):
        def some(i, _):
            for u in range(16):
                c = i * 16 + u
                s_ref[c, pl.ds(at, count), :] = turned[
                    pl.ds(c * turn_stride + at, count), :
                ].astype(jnp.bfloat16)
            return 0

        lax.fori_loop(0, channels // 16, some, 0)

    def main_part(i, _):
        starts = [(h * paired + i * 2 + p) * main_stride for p in range(2) for h in range(2)]
        y = dft(gather(late, starts, main))
        for p in range(2):
            cols = slice(p * LANES, (p + 1) * LANES)
            re, im = y[:channels, cols], y[channels:, cols]
            turn(i * 2 + p, jnp.where(low, re, pltpu.roll(im, LANES // 2, 1)))
            turn(i * 2 + p + paired, jnp.where(low, pltpu.roll(re, LANES // 2, 1), im))
        return 0

    lax.fori_loop(0, paired // 2, main_part, 0, unroll=4)
    pack(0, antennas)
    for tile in range(tiles):
        polyphase(frames, w_ref, tile, 8, first // 8 - 1, taps, store_rest)

    before()
    last = joined.at[:, pl.ds(samples, halo)]
    landing = joined.at[:, pl.ds(0, halo)]

    @pl.when(t < tms - 1)
    def _():
        pltpu.make_async_remote_copy(
            src_ref=last,
            dst_ref=landing,
            send_sem=halo_sems.at[0],
            recv_sem=halo_sems.at[1],
            device_id=(lax.rem(t + 1, tms), f),
            device_id_type=MESH,
        ).start()

    between()

    @pl.when(t > 0)
    def _():
        pltpu.make_async_copy(landing, landing, halo_sems.at[1]).wait()

    for tile in range(tiles):
        polyphase(frames, w_ref, tile, 0, 1, taps, store_rest)

    def rest_part(i, _):
        starts = [(h * eighth + i * 2 + p) * rest_stride for p in range(2) for h in range(4)]
        y = dft(gather(early, starts, first))
        for p in range(2):
            cols = slice(p * LANES, (p + 1) * LANES)
            re, im = y[:channels, cols], y[channels:, cols]
            row = antennas + i * 2 + p
            turn(row, jnp.where(quarter, re, pltpu.roll(im, LANES // 4, 1)))
            turn(row + eighth, jnp.where(quarter, pltpu.roll(re, LANES - LANES // 4, 1), im))
        return 0

    lax.fori_loop(0, eighth // 2, rest_part, 0, unroll=4)
    pack(antennas, paired)

    @pl.when(t < tms - 1)
    def _():
        pltpu.make_async_copy(last, last, halo_sems.at[0]).wait()


def correlate_kernel(
    tms,
    groups,
    scale,
    v_ref,
    window_ref,
    table_ref,
    r_ref,
    joined,
    w_ref,
    c_ref,
    early,
    late,
    turned,
    s_ref,
    x_ref,
    right,
    left,
    outs,
    load_sems,
    halo_sems,
    send1,
    recv1,
    send2,
    recv2,
    send3,
    recv3,
):
    t, f = lax.axis_index("tm"), lax.axis_index("freq")
    g, k = f // 2, f % 2
    half = tms // 2
    peers = tms * groups
    rows = s_ref.shape[1]
    ants = 2 * rows // 3
    sibling = (t, 2 * g + 1 - k)
    mine = g // 2 % half
    my_high = g // (2 * half)

    halo = joined.shape[1] - v_ref.shape[1]
    loads = [
        pltpu.make_async_copy(source, target, load_sems.at[i])
        for i, (source, target) in enumerate(
            (
                (v_ref, joined.at[:, pl.ds(halo, v_ref.shape[1])]),
                (window_ref, w_ref),
                (table_ref, c_ref),
            )
        )
    ]
    for load in loads:
        load.start()
    barrier = pltpu.get_barrier_semaphore()

    def greet(n):
        tt, gg = lax.rem(t + n // groups, tms), lax.rem(g + n % groups, groups)
        to = jnp.where(n == 0, 2 * g + 1 - k, 2 * gg + k)
        pl.semaphore_signal(barrier, inc=1, device_id=(tt, to), device_id_type=MESH)
        return 0

    for j in range(half):
        pl.semaphore_signal(
            barrier, inc=1, device_id=(half * k + j, 2 * g + 1 - k), device_id_type=MESH
        )

    def await_greetings():
        pl.semaphore_wait(barrier, peers + jnp.where(k == t // half, 0, tms))

    def send_phase(n, first_row, row_count):
        def send_block(i, _):
            tt = lax.rem(t + i // 2, tms)
            part = lax.rem(mine + 2 * half - tt % half - n // 2, half)
            high = lax.rem(my_high + tt // half + n % 2, 2)
            gg = (high * half + part) * 2 + lax.rem(g + i, 2)
            some = pl.ds(first_row, row_count)
            src = s_ref.at[gg * tms + tt, some]
            dst = x_ref.at[k, mine, my_high, g % 2, t, some]
            here = (tt == t) & (gg == g)

            @pl.when(here)
            def _():
                pltpu.make_async_copy(src, dst, recv1.at[n]).start()

            @pl.when(jnp.logical_not(here))
            def _():
                pltpu.make_async_remote_copy(
                    src_ref=src,
                    dst_ref=dst,
                    send_sem=send1,
                    recv_sem=recv1.at[n],
                    device_id=(tt, 2 * gg + k),
                    device_id_type=MESH,
                ).start()

            return 0

        lax.fori_loop(0, 2 * tms, send_block, 0)
        return 0

    def send_phases(first, last, first_row, row_count):
        lax.fori_loop(first, last, lambda n, _: send_phase(n, first_row, row_count), 0)

    channelize(
        v_ref,
        w_ref,
        c_ref,
        s_ref,
        joined,
        early,
        late,
        turned,
        loads,
        halo_sems,
        t,
        f,
        tms,
        greet,
        peers,
        await_greetings,
        lambda: send_phases(0, EARLY, 0, ants),
    )
    send_phases(0, EARLY, ants, rows - ants)
    send_phases(EARLY, tms, 0, rows)

    wide = tms * LANES
    lane = lax.broadcasted_iota(jnp.int32, (ants, LANES), 1)
    low = lane < LANES // 2
    quarter = lane % (LANES // 2) < LANES // 4
    block = ants * 4
    own = block // 2
    slot = t % half
    dims = (((1,), (1,)), ((), ()))

    def place(n):
        return lax.rem(my_high + t // half + n % 2, 2), lax.rem(mine + t + n // 2, half)

    def phase(n, _):
        high, part = place(n)
        arrived = x_ref.at[k, part, high]
        pltpu.make_async_copy(arrived, arrived, recv1.at[n]).wait()
        pltpu.make_async_remote_copy(
            src_ref=arrived,
            dst_ref=arrived,
            send_sem=send3,
            recv_sem=recv3.at[n],
            device_id=sibling,
            device_id_type=MESH,
        ).start()

        def assemble(kk, mine_too):
            for low_g in range(2):
                base = pl.multiple_of((2 * low_g + kk) * ants, ants)

                def put(at, cols, value, turned_value):
                    count = value.shape[0]
                    right[n, pl.ds(base + at, count), cols] = value
                    if mine_too:
                        left[n, 0, low_g * ants + at : low_g * ants + at + count, cols] = value
                        left[n, 1, low_g * ants + at : low_g * ants + at + count, cols] = (
                            turned_value(value)
                        )

                def turn_wide(v):
                    v = pltpu.roll(v, LANES // 2, 1)
                    return jnp.where(low[: v.shape[0]], v, -v)

                def turn_narrow(v):
                    ahead = pltpu.roll(v, LANES - LANES // 4, 1)
                    behind = pltpu.roll(v, LANES // 4, 1)
                    return jnp.where(quarter[: v.shape[0]], ahead, -behind)

                for tt in range(tms):
                    cols = slice(tt * LANES, (tt + 1) * LANES)
                    put(0, cols, x_ref[kk, part, high, low_g, tt, :ants, :], turn_wide)
                for tt in range(0, tms, 2):
                    h0 = x_ref[kk, part, high, low_g, tt, ants:, :]
                    h1 = x_ref[kk, part, high, low_g, tt + 1, ants:, :]
                    some = low[: ants // 2]
                    cols = slice(wide + tt // 2 * LANES, wide + (tt // 2 + 1) * LANES)
                    top = jnp.where(some, h0, pltpu.roll(h1, LANES // 2, 1))
                    put(0, cols, top, turn_narrow)
                    bottom = jnp.where(some, pltpu.roll(h0, LANES // 2, 1), h1)
                    put(ants // 2, cols, bottom, turn_narrow)

        assemble(k, True)

        def piece(row, row_count, col, col_count):
            value = lax.dot_general(
                left[pl.ds(row, row_count)].reshape(row_count * block, -1),
                right[pl.ds(col, col_count)].reshape(col_count * block, -1),
                dims,
                preferred_element_type=jnp.float32,
            )
            value = (value * scale).astype(jnp.bfloat16)
            value = value.reshape(row_count, 2, 2, ants, col_count * block)
            for r in range(row_count):
                to_high, to_part = place(row + r)
                target = to_high * half + to_part
                here = (t == target) & (k == t // half)
                for c in range(col_count):
                    at_high, at_part = place(col + c)
                    cols = pl.ds(pl.multiple_of((at_high * half + at_part) * block, block), block)
                    outs[row + r, :, :, :, cols] = value[r, :, :, :, c * block : (c + 1) * block]
                    src = outs.at[row + r, :, :, :, cols]
                    dst = r_ref.at[:, slot, :, k, :, cols]

                    @pl.when(here)
                    def _():
                        pltpu.make_async_copy(src, dst, recv2).start()

                    @pl.when(jnp.logical_not(here))
                    def _():
                        pltpu.make_async_remote_copy(
                            src_ref=src,
                            dst_ref=dst,
                            send_sem=send2,
                            recv_sem=recv2,
                            device_id=(target, 2 * g + t // half),
                            device_id_type=MESH,
                        ).start()

        def row_pair(i, _):
            piece(n, 1, 2 * i, 2)
            return 0

        def column_pair(i, _):
            piece(2 * i, 2, n, 1)
            return 0

        lax.fori_loop(0, n // 2, row_pair, 0)

        @pl.when(n % 2 == 1)
        def _():
            piece(n, 1, n - 1, 1)

        other = x_ref.at[1 - k, part, high]
        pltpu.make_async_copy(other, other, recv3.at[n]).wait()
        assemble(1 - k, False)
        lax.fori_loop(0, (n + 1) // 2, column_pair, 0)

        @pl.when(n % 2 == 0)
        def _():
            piece(n, 1, n, 1)

        return 0

    lax.fori_loop(0, tms, phase, 0)
    pltpu.make_async_copy(r_ref, r_ref, recv2).wait()

    pltpu.make_async_copy(x_ref.at[k], x_ref.at[k], send3).wait()
    sent = s_ref.at[pl.ds(0, peers - 1)]
    pltpu.make_async_copy(sent, sent, send1).wait()

    @pl.when(k == t // half)
    def _():
        kept = outs.at[pl.ds(0, tms - 1)]
        pltpu.make_async_copy(kept, kept, send2).wait()

    @pl.when(k != t // half)
    def _():
        pltpu.make_async_copy(outs, outs, send2).wait()


def cast_kernel(pieces, r_ref, o_ref, taken, wide, read_sems, write_sems):
    rows = r_ref.shape[0] // pieces
    slices = [pl.ds(i * rows, rows) for i in range(pieces)]
    reads = [
        pltpu.make_async_copy(r_ref.at[some], taken.at[some], read_sems.at[i])
        for i, some in enumerate(slices)
    ]
    writes = [
        pltpu.make_async_copy(wide.at[some], o_ref.at[some], write_sems.at[i])
        for i, some in enumerate(slices)
    ]
    for read in reads:
        read.start()
    for some, read, write in zip(slices, reads, writes):
        read.wait()
        wide[some] = taken[some].astype(jnp.float32)
        write.start()
    for write in writes:
        write.wait()


def cast(values):
    pieces = 8
    anywhere = pl.BlockSpec(memory_space=pl.ANY)
    return pl.pallas_call(
        functools.partial(cast_kernel, pieces),
        out_shape=jax.ShapeDtypeStruct(values.shape, jnp.float32),
        in_specs=[anywhere],
        out_specs=anywhere,
        scratch_shapes=[
            pltpu.VMEM(values.shape, jnp.bfloat16),
            pltpu.VMEM(values.shape, jnp.float32),
            pltpu.SemaphoreType.DMA((pieces,)),
            pltpu.SemaphoreType.DMA((pieces,)),
        ],
        compiler_params=pltpu.CompilerParams(vmem_limit_bytes=60 << 20),
    )(values)


def local(voltages, window):
    tms, freqs = lax.axis_size("tm"), lax.axis_size("freq")
    groups = freqs // 2
    half = tms // 2
    taps, period = window.shape
    antennas, samples = voltages.shape
    spec_here = samples // period
    channels = period // 2
    assert channels == tms * groups
    rows = antennas * 3 // 2
    total = antennas * freqs
    row_count = total // tms
    depth = 2 * spec_here * tms
    result = pl.pallas_call(
        functools.partial(correlate_kernel, tms, groups, (spec_here * tms) ** (-0.5)),
        out_shape=jax.ShapeDtypeStruct((2, half, 2, 2, antennas, total), jnp.bfloat16),
        in_specs=[pl.BlockSpec(memory_space=pl.ANY)] * 3,
        out_specs=pl.BlockSpec(memory_space=pl.ANY),
        scratch_shapes=[
            pltpu.VMEM((antennas, samples + (taps - 1) * period), jnp.bfloat16),
            pltpu.VMEM(window.shape, jnp.float32),
            pltpu.VMEM((4 * channels, period), jnp.bfloat16),
            pltpu.VMEM((period // LANES, antennas * (spec_here // 3 + 1), LANES), jnp.float32),
            pltpu.VMEM((period // LANES, antennas * (2 * spec_here // 3 + 1), LANES), jnp.float32),
            pltpu.VMEM((channels * (rows + 1), LANES), jnp.float32),
            pltpu.VMEM((channels, rows, LANES), jnp.bfloat16),
            pltpu.VMEM((2, half, 2, 2, tms, rows, LANES), jnp.bfloat16),
            pltpu.VMEM((tms, row_count, depth), jnp.bfloat16),
            pltpu.VMEM((tms, 2, row_count // 2, depth), jnp.bfloat16),
            pltpu.VMEM((tms, 2, 2, antennas, total), jnp.bfloat16),
            pltpu.SemaphoreType.DMA((3,)),
            pltpu.SemaphoreType.DMA((2,)),
            pltpu.SemaphoreType.DMA,
            pltpu.SemaphoreType.DMA((tms,)),
            pltpu.SemaphoreType.DMA,
            pltpu.SemaphoreType.DMA,
            pltpu.SemaphoreType.DMA,
            pltpu.SemaphoreType.DMA((tms,)),
        ],
        compiler_params=pltpu.CompilerParams(
            collective_id=0, has_side_effects=True, vmem_limit_bytes=60 << 20
        ),
        cost_estimate=pl.CostEstimate(
            flops=2 * 2 * (total // 2) * total * depth, bytes_accessed=8 << 20, transcendentals=0
        ),
    )(voltages, window, jnp.asarray(dft_table(period, channels)))
    return cast(result.reshape(2 * half * row_count, total)).reshape(2, half, row_count, total)


def solution(mesh):
    return jax.shard_map(
        local,
        mesh=mesh,
        in_specs=(P("freq", "tm"), P()),
        out_specs=P(None, "freq", "tm", None),
        check_vma=False,
    )
```

```python
import functools
import math

import jax
import jax.numpy as jnp
import numpy as np
from jax import lax
from jax.experimental import pallas as pl
from jax.experimental.pallas import tpu as pltpu
from jax.sharding import PartitionSpec as P

MESH = pl.DeviceIdType.MESH
LANES = 128
EARLY = 1


def dft_table(length, channels):
    sample, channel = np.arange(length), np.arange(channels)
    phase = (channel[:, None] * sample[None, :] % length) * (2.0 * math.pi / length)
    rows = np.concatenate([np.cos(phase), -np.sin(phase)], axis=0) * length ** (-0.5)
    high = rows.astype(jnp.bfloat16)
    low = (rows - high.astype(np.float64)).astype(jnp.bfloat16)
    return np.concatenate([high, low], axis=0)


def polyphase(frames, w_ref, tile, first, groups, taps, store):
    cols = slice(tile * LANES, (tile + 1) * LANES)
    weights = [w_ref[k : k + 1, cols] for k in range(taps)]

    def group(i, held):
        held = list(held)
        for u in range(8):
            at = first + i * 8 + u
            held.append(frames(at + taps - 1, tile))
            value = weights[0] * held[0]
            for k in range(1, taps):
                value = value + weights[k] * held[k]
            held.pop(0)
            store(at, tile, value)
        return tuple(held)

    lax.fori_loop(0, groups, group, tuple(frames(first + j, tile) for j in range(taps - 1)))


def channelize(
    v_ref, w_ref, c_ref, s_ref, joined, early, late, turned, loads, halo_sems, t, between
):
    taps, period = w_ref.shape
    antennas, samples = v_ref.shape
    spec = samples // period
    first, main = spec // 3, 2 * spec // 3
    tiles = period // LANES
    channels = period // 2
    halo = (taps - 1) * period
    paired = antennas // 2
    eighth = antennas // 4
    main_stride, rest_stride = main + 1, first + 1
    turn_stride = s_ref.shape[1] + 1

    def frames(j, tile):
        at = pl.multiple_of(j * period + tile * LANES, LANES)
        return joined[:, pl.ds(at, LANES)].astype(jnp.float32)

    def store_main(at, tile, value):
        for h in range(2):
            rows = pl.ds(h * paired * main_stride + at - first, paired, stride=main_stride)
            late[tile, rows, :] = value[h * paired : (h + 1) * paired]

    def store_rest(at, tile, value):
        for h in range(4):
            rows = pl.ds(h * eighth * rest_stride + at, eighth, stride=rest_stride)
            early[tile, rows, :] = value[h * eighth : (h + 1) * eighth]

    @pl.when(t == 0)
    def _():
        joined[:, :halo] = jnp.zeros((antennas, halo), jnp.bfloat16)

    for load in loads:
        load.wait()
    for tile in range(tiles):
        polyphase(frames, w_ref, tile, first, main // 8, taps, store_main)

    lane = lax.broadcasted_iota(jnp.int32, (channels, LANES), 1)
    low = lane < LANES // 2
    quarter = lane % (LANES // 2) < LANES // 4
    dims = (((1,), (1,)), ((), ()))

    def dft(x):
        high = x.astype(jnp.bfloat16)
        rest = (x - high.astype(jnp.float32)).astype(jnp.bfloat16)
        y = lax.dot_general(c_ref[...], high, dims, preferred_element_type=jnp.float32)
        z = lax.dot_general(
            c_ref[: 2 * channels, :], rest, dims, preferred_element_type=jnp.float32
        )
        return y[: 2 * channels] + y[2 * channels :] + z

    def gather(ref, starts, count):
        return jnp.concatenate(
            [
                jnp.concatenate([ref[tile, pl.ds(at, count), :] for at in starts], axis=0)
                for tile in range(tiles)
            ],
            axis=1,
        )

    def turn(row, value):
        turned[pl.ds(row, channels, stride=turn_stride), :] = value

    def pack(at, count):
        def some(i, _):
            for u in range(16):
                c = i * 16 + u
                s_ref[c, pl.ds(at, count), :] = turned[
                    pl.ds(c * turn_stride + at, count), :
                ].astype(jnp.bfloat16)
            return 0

        lax.fori_loop(0, channels // 16, some, 0)

    def main_part(i, _):
        starts = [(h * paired + i * 2 + p) * main_stride for p in range(2) for h in range(2)]
        y = dft(gather(late, starts, main))
        for p in range(2):
            cols = slice(p * LANES, (p + 1) * LANES)
            re, im = y[:channels, cols], y[channels:, cols]
            turn(i * 2 + p, jnp.where(low, re, pltpu.roll(im, LANES // 2, 1)))
            turn(i * 2 + p + paired, jnp.where(low, pltpu.roll(re, LANES // 2, 1), im))
        return 0

    lax.fori_loop(0, paired // 2, main_part, 0, unroll=4)
    pack(0, antennas)
    for tile in range(tiles):
        polyphase(frames, w_ref, tile, 8, first // 8 - 1, taps, store_rest)

    between()

    @pl.when(t > 0)
    def _():
        landing = joined.at[:, pl.ds(0, halo)]
        pltpu.make_async_copy(landing, landing, halo_sems.at[1]).wait()

    for tile in range(tiles):
        polyphase(frames, w_ref, tile, 0, 1, taps, store_rest)

    def rest_part(i, _):
        starts = [(h * eighth + i * 2 + p) * rest_stride for p in range(2) for h in range(4)]
        y = dft(gather(early, starts, first))
        for p in range(2):
            cols = slice(p * LANES, (p + 1) * LANES)
            re, im = y[:channels, cols], y[channels:, cols]
            row = antennas + i * 2 + p
            turn(row, jnp.where(quarter, re, pltpu.roll(im, LANES // 4, 1)))
            turn(row + eighth, jnp.where(quarter, pltpu.roll(re, LANES - LANES // 4, 1), im))
        return 0

    lax.fori_loop(0, eighth // 2, rest_part, 0, unroll=4)
    pack(antennas, paired)


def correlate_kernel(
    tms,
    groups,
    scale,
    v_ref,
    window_ref,
    table_ref,
    r_ref,
    joined,
    w_ref,
    c_ref,
    early,
    late,
    turned,
    s_ref,
    x_ref,
    right,
    left,
    outs,
    ready,
    load_sems,
    halo_sems,
    send1,
    recv1,
    send2,
    recv2,
    send3,
    recv3,
):
    t, f = lax.axis_index("tm"), lax.axis_index("freq")
    g, k = f // 2, f % 2
    half = tms // 2
    peers = tms * groups
    rows = s_ref.shape[1]
    ants = 2 * rows // 3
    sibling = (t, 2 * g + 1 - k)
    mine = g // 2 % half
    my_high = g // (2 * half)

    halo = joined.shape[1] - v_ref.shape[1]
    loads = [
        pltpu.make_async_copy(source, target, load_sems.at[i])
        for i, (source, target) in enumerate(
            (
                (v_ref, joined.at[:, pl.ds(halo, v_ref.shape[1])]),
                (window_ref, w_ref),
                (table_ref, c_ref),
            )
        )
    ]
    for load in loads:
        load.start()
    barrier = pltpu.get_barrier_semaphore()

    def greet(to):
        pl.semaphore_signal(barrier, inc=1, device_id=to, device_id_type=MESH)

    column = [(lax.rem(t + i, tms), 2 * g + k) for i in range(1, tms)]
    for i in range(1, groups):
        greet((t, 2 * lax.rem(g + i, groups) + k))
    for to in column + [sibling] + [(half * k + j, 2 * g + 1 - k) for j in range(half)]:
        greet(to)
    pl.semaphore_wait(barrier, groups + tms - 1 + jnp.where(k == t // half, 0, tms))
    for to in column:
        pl.semaphore_signal(ready, inc=1, device_id=to, device_id_type=MESH)

    last = v_ref.at[:, pl.ds(v_ref.shape[1] - halo, halo)]
    landing = joined.at[:, pl.ds(0, halo)]

    @pl.when(t < tms - 1)
    def _():
        pltpu.make_async_remote_copy(
            src_ref=last,
            dst_ref=landing,
            send_sem=halo_sems.at[0],
            recv_sem=halo_sems.at[1],
            device_id=(lax.rem(t + 1, tms), f),
            device_id_type=MESH,
        ).start()

    def send_phase(n, first_row, row_count):
        def send_block(i, _):
            tt = lax.rem(t + i // 2, tms)
            part = lax.rem(mine + 2 * half - tt % half - n // 2, half)
            high = lax.rem(my_high + tt // half + n % 2, 2)
            gg = (high * half + part) * 2 + lax.rem(g + i, 2)
            some = pl.ds(first_row, row_count)
            src = s_ref.at[gg * tms + tt, some]
            dst = x_ref.at[k, mine, my_high, g % 2, t, some]
            here = (tt == t) & (gg == g)

            @pl.when(here)
            def _():
                pltpu.make_async_copy(src, dst, recv1.at[n]).start()

            @pl.when(jnp.logical_not(here))
            def _():
                pltpu.make_async_remote_copy(
                    src_ref=src,
                    dst_ref=dst,
                    send_sem=send1,
                    recv_sem=recv1.at[n],
                    device_id=(tt, 2 * gg + k),
                    device_id_type=MESH,
                ).start()

            return 0

        lax.fori_loop(0, 2 * tms, send_block, 0)
        return 0

    def send_phases(first, last, first_row, row_count):
        lax.fori_loop(first, last, lambda n, _: send_phase(n, first_row, row_count), 0)

    def send_early():
        pl.semaphore_wait(ready, tms - 1)
        send_phases(0, EARLY, 0, ants)

    channelize(
        v_ref,
        w_ref,
        c_ref,
        s_ref,
        joined,
        early,
        late,
        turned,
        loads,
        halo_sems,
        t,
        send_early,
    )
    send_phases(0, EARLY, ants, rows - ants)
    send_phases(EARLY, tms, 0, rows)

    wide = tms * LANES
    lane = lax.broadcasted_iota(jnp.int32, (ants, LANES), 1)
    low = lane < LANES // 2
    quarter = lane % (LANES // 2) < LANES // 4
    block = ants * 4
    own = block // 2
    slot = t % half
    dims = (((1,), (1,)), ((), ()))

    def place(n):
        return lax.rem(my_high + t // half + n % 2, 2), lax.rem(mine + t + n // 2, half)

    def phase(n, _):
        high, part = place(n)
        arrived = x_ref.at[k, part, high]
        pltpu.make_async_copy(arrived, arrived, recv1.at[n]).wait()
        pltpu.make_async_remote_copy(
            src_ref=arrived,
            dst_ref=arrived,
            send_sem=send3,
            recv_sem=recv3.at[n],
            device_id=sibling,
            device_id_type=MESH,
        ).start()

        def assemble(kk, mine_too):
            for low_g in range(2):
                base = pl.multiple_of((2 * low_g + kk) * ants, ants)

                def put(at, cols, value, turned_value):
                    count = value.shape[0]
                    right[n, pl.ds(base + at, count), cols] = value
                    if mine_too:
                        left[n, 0, low_g * ants + at : low_g * ants + at + count, cols] = value
                        left[n, 1, low_g * ants + at : low_g * ants + at + count, cols] = (
                            turned_value(value)
                        )

                def turn_wide(v):
                    v = pltpu.roll(v, LANES // 2, 1)
                    return jnp.where(low[: v.shape[0]], v, -v)

                def turn_narrow(v):
                    ahead = pltpu.roll(v, LANES - LANES // 4, 1)
                    behind = pltpu.roll(v, LANES // 4, 1)
                    return jnp.where(quarter[: v.shape[0]], ahead, -behind)

                for tt in range(tms):
                    cols = slice(tt * LANES, (tt + 1) * LANES)
                    put(0, cols, x_ref[kk, part, high, low_g, tt, :ants, :], turn_wide)
                for tt in range(0, tms, 2):
                    h0 = x_ref[kk, part, high, low_g, tt, ants:, :]
                    h1 = x_ref[kk, part, high, low_g, tt + 1, ants:, :]
                    some = low[: ants // 2]
                    cols = slice(wide + tt // 2 * LANES, wide + (tt // 2 + 1) * LANES)
                    top = jnp.where(some, h0, pltpu.roll(h1, LANES // 2, 1))
                    put(0, cols, top, turn_narrow)
                    bottom = jnp.where(some, pltpu.roll(h0, LANES // 2, 1), h1)
                    put(ants // 2, cols, bottom, turn_narrow)

        assemble(k, True)

        def piece(row, row_count, col, col_count):
            value = lax.dot_general(
                left[pl.ds(row, row_count)].reshape(row_count * block, -1),
                right[pl.ds(col, col_count)].reshape(col_count * block, -1),
                dims,
                preferred_element_type=jnp.float32,
            )
            value = (value * scale).astype(jnp.bfloat16)
            value = value.reshape(row_count, 2, 2, ants, col_count * block)
            for r in range(row_count):
                to_high, to_part = place(row + r)
                target = to_high * half + to_part
                here = (t == target) & (k == t // half)
                for c in range(col_count):
                    at_high, at_part = place(col + c)
                    cols = pl.ds(pl.multiple_of((at_high * half + at_part) * block, block), block)
                    outs[row + r, :, :, :, cols] = value[r, :, :, :, c * block : (c + 1) * block]
                    src = outs.at[row + r, :, :, :, cols]
                    dst = r_ref.at[:, slot, :, k, :, cols]

                    @pl.when(here)
                    def _():
                        pltpu.make_async_copy(src, dst, recv2).start()

                    @pl.when(jnp.logical_not(here))
                    def _():
                        pltpu.make_async_remote_copy(
                            src_ref=src,
                            dst_ref=dst,
                            send_sem=send2,
                            recv_sem=recv2,
                            device_id=(target, 2 * g + t // half),
                            device_id_type=MESH,
                        ).start()

        def row_pair(i, _):
            piece(n, 1, 2 * i, 2)
            return 0

        def column_pair(i, _):
            piece(2 * i, 2, n, 1)
            return 0

        lax.fori_loop(0, n // 2, row_pair, 0)

        @pl.when(n % 2 == 1)
        def _():
            piece(n, 1, n - 1, 1)

        other = x_ref.at[1 - k, part, high]
        pltpu.make_async_copy(other, other, recv3.at[n]).wait()
        assemble(1 - k, False)
        lax.fori_loop(0, (n + 1) // 2, column_pair, 0)

        @pl.when(n % 2 == 0)
        def _():
            piece(n, 1, n, 1)

        return 0

    lax.fori_loop(0, tms, phase, 0)
    pltpu.make_async_copy(r_ref, r_ref, recv2).wait()

    @pl.when(t < tms - 1)
    def _():
        pltpu.make_async_copy(landing, landing, halo_sems.at[0]).wait()

    pltpu.make_async_copy(x_ref.at[k], x_ref.at[k], send3).wait()
    sent = s_ref.at[pl.ds(0, peers - 1)]
    pltpu.make_async_copy(sent, sent, send1).wait()

    @pl.when(k == t // half)
    def _():
        kept = outs.at[pl.ds(0, tms - 1)]
        pltpu.make_async_copy(kept, kept, send2).wait()

    @pl.when(k != t // half)
    def _():
        pltpu.make_async_copy(outs, outs, send2).wait()


def cast_kernel(pieces, r_ref, o_ref, taken, wide, read_sems, write_sems):
    rows = r_ref.shape[0] // pieces
    slices = [pl.ds(i * rows, rows) for i in range(pieces)]
    reads = [
        pltpu.make_async_copy(r_ref.at[some], taken.at[some], read_sems.at[i])
        for i, some in enumerate(slices)
    ]
    writes = [
        pltpu.make_async_copy(wide.at[some], o_ref.at[some], write_sems.at[i])
        for i, some in enumerate(slices)
    ]
    for read in reads:
        read.start()
    for some, read, write in zip(slices, reads, writes):
        read.wait()
        wide[some] = taken[some].astype(jnp.float32)
        write.start()
    for write in writes:
        write.wait()


def cast(values):
    pieces = 8
    anywhere = pl.BlockSpec(memory_space=pl.ANY)
    return pl.pallas_call(
        functools.partial(cast_kernel, pieces),
        out_shape=jax.ShapeDtypeStruct(values.shape, jnp.float32),
        in_specs=[anywhere],
        out_specs=anywhere,
        scratch_shapes=[
            pltpu.VMEM(values.shape, jnp.bfloat16),
            pltpu.VMEM(values.shape, jnp.float32),
            pltpu.SemaphoreType.DMA((pieces,)),
            pltpu.SemaphoreType.DMA((pieces,)),
        ],
        compiler_params=pltpu.CompilerParams(vmem_limit_bytes=60 << 20),
    )(values)


def local(voltages, window):
    tms, freqs = lax.axis_size("tm"), lax.axis_size("freq")
    groups = freqs // 2
    half = tms // 2
    taps, period = window.shape
    antennas, samples = voltages.shape
    spec_here = samples // period
    channels = period // 2
    assert channels == tms * groups
    rows = antennas * 3 // 2
    total = antennas * freqs
    row_count = total // tms
    depth = 2 * spec_here * tms
    result = pl.pallas_call(
        functools.partial(correlate_kernel, tms, groups, (spec_here * tms) ** (-0.5)),
        out_shape=jax.ShapeDtypeStruct((2, half, 2, 2, antennas, total), jnp.bfloat16),
        in_specs=[pl.BlockSpec(memory_space=pl.ANY)] * 3,
        out_specs=pl.BlockSpec(memory_space=pl.ANY),
        scratch_shapes=[
            pltpu.VMEM((antennas, samples + (taps - 1) * period), jnp.bfloat16),
            pltpu.VMEM(window.shape, jnp.float32),
            pltpu.VMEM((4 * channels, period), jnp.bfloat16),
            pltpu.VMEM((period // LANES, antennas * (spec_here // 3 + 1), LANES), jnp.float32),
            pltpu.VMEM((period // LANES, antennas * (2 * spec_here // 3 + 1), LANES), jnp.float32),
            pltpu.VMEM((channels * (rows + 1), LANES), jnp.float32),
            pltpu.VMEM((channels, rows, LANES), jnp.bfloat16),
            pltpu.VMEM((2, half, 2, 2, tms, rows, LANES), jnp.bfloat16),
            pltpu.VMEM((tms, row_count, depth), jnp.bfloat16),
            pltpu.VMEM((tms, 2, row_count // 2, depth), jnp.bfloat16),
            pltpu.VMEM((tms, 2, 2, antennas, total), jnp.bfloat16),
            pltpu.SemaphoreType.REGULAR,
            pltpu.SemaphoreType.DMA((3,)),
            pltpu.SemaphoreType.DMA((2,)),
            pltpu.SemaphoreType.DMA,
            pltpu.SemaphoreType.DMA((tms,)),
            pltpu.SemaphoreType.DMA,
            pltpu.SemaphoreType.DMA,
            pltpu.SemaphoreType.DMA,
            pltpu.SemaphoreType.DMA((tms,)),
        ],
        compiler_params=pltpu.CompilerParams(
            collective_id=0, has_side_effects=True, vmem_limit_bytes=60 << 20
        ),
        cost_estimate=pl.CostEstimate(
            flops=2 * 2 * (total // 2) * total * depth, bytes_accessed=8 << 20, transcendentals=0
        ),
    )(voltages, window, jnp.asarray(dft_table(period, channels)))
    return cast(result.reshape(2 * half * row_count, total)).reshape(2, half, row_count, total)


def solution(mesh):
    return jax.shard_map(
        local,
        mesh=mesh,
        in_specs=(P("freq", "tm"), P()),
        out_specs=P(None, "freq", "tm", None),
        check_vma=False,
    )
```

```python
import functools
import math

import jax
import jax.numpy as jnp
import numpy as np
from jax import lax
from jax.experimental import pallas as pl
from jax.experimental.pallas import tpu as pltpu
from jax.sharding import PartitionSpec as P

MESH = pl.DeviceIdType.MESH
LANES = 128
EARLY = 1


def dft_table(length, channels):
    sample, channel = np.arange(length), np.arange(channels)
    phase = (channel[:, None] * sample[None, :] % length) * (2.0 * math.pi / length)
    rows = np.concatenate([np.cos(phase), -np.sin(phase)], axis=0) * length ** (-0.5)
    high = rows.astype(jnp.bfloat16)
    low = (rows - high.astype(np.float64)).astype(jnp.bfloat16)
    return np.concatenate([high, low], axis=0)


def polyphase(frames, w_ref, tile, first, groups, taps, store):
    cols = slice(tile * LANES, (tile + 1) * LANES)
    weights = [w_ref[k : k + 1, cols] for k in range(taps)]

    def group(i, held):
        held = list(held)
        for u in range(8):
            at = first + i * 8 + u
            held.append(frames(at + taps - 1, tile))
            value = weights[0] * held[0]
            for k in range(1, taps):
                value = value + weights[k] * held[k]
            held.pop(0)
            store(at, tile, value)
        return tuple(held)

    lax.fori_loop(0, groups, group, tuple(frames(first + j, tile) for j in range(taps - 1)))


def channelize(
    v_ref, w_ref, c_ref, s_ref, joined, early, late, turned, loads, halo_sems, t, between
):
    taps, period = w_ref.shape
    antennas, samples = v_ref.shape
    spec = samples // period
    first, main = spec // 3, 2 * spec // 3
    tiles = period // LANES
    channels = period // 2
    halo = (taps - 1) * period
    paired = antennas // 2
    eighth = antennas // 4
    main_stride, rest_stride = main + 1, first + 1
    turn_stride = s_ref.shape[1] + 1

    def frames(j, tile):
        at = pl.multiple_of(j * period + tile * LANES, LANES)
        return joined[:, pl.ds(at, LANES)].astype(jnp.float32)

    def store_main(at, tile, value):
        for h in range(2):
            rows = pl.ds(h * paired * main_stride + at - first, paired, stride=main_stride)
            late[tile, rows, :] = value[h * paired : (h + 1) * paired]

    def store_rest(at, tile, value):
        for h in range(4):
            rows = pl.ds(h * eighth * rest_stride + at, eighth, stride=rest_stride)
            early[tile, rows, :] = value[h * eighth : (h + 1) * eighth]

    @pl.when(t == 0)
    def _():
        joined[:, :halo] = jnp.zeros((antennas, halo), jnp.bfloat16)

    for load in loads:
        load.wait()
    for tile in range(tiles):
        polyphase(frames, w_ref, tile, first, main // 8, taps, store_main)

    lane = lax.broadcasted_iota(jnp.int32, (channels, LANES), 1)
    low = lane < LANES // 2
    quarter = lane % (LANES // 2) < LANES // 4
    dims = (((1,), (1,)), ((), ()))

    def dft(x):
        high = x.astype(jnp.bfloat16)
        rest = (x - high.astype(jnp.float32)).astype(jnp.bfloat16)
        y = lax.dot_general(c_ref[...], high, dims, preferred_element_type=jnp.float32)
        z = lax.dot_general(
            c_ref[: 2 * channels, :], rest, dims, preferred_element_type=jnp.float32
        )
        return y[: 2 * channels] + y[2 * channels :] + z

    def gather(ref, starts, count):
        return jnp.concatenate(
            [
                jnp.concatenate([ref[tile, pl.ds(at, count), :] for at in starts], axis=0)
                for tile in range(tiles)
            ],
            axis=1,
        )

    def turn(row, value):
        turned[pl.ds(row, channels, stride=turn_stride), :] = value

    def pack(at, count):
        def some(i, _):
            for u in range(16):
                c = i * 16 + u
                s_ref[c, pl.ds(at, count), :] = turned[
                    pl.ds(c * turn_stride + at, count), :
                ].astype(jnp.bfloat16)
            return 0

        lax.fori_loop(0, channels // 16, some, 0)

    def main_part(i, _):
        starts = [(h * paired + i * 2 + p) * main_stride for p in range(2) for h in range(2)]
        y = dft(gather(late, starts, main))
        for p in range(2):
            cols = slice(p * LANES, (p + 1) * LANES)
            re, im = y[:channels, cols], y[channels:, cols]
            turn(i * 2 + p, jnp.where(low, re, pltpu.roll(im, LANES // 2, 1)))
            turn(i * 2 + p + paired, jnp.where(low, pltpu.roll(re, LANES // 2, 1), im))
        return 0

    lax.fori_loop(0, paired // 2, main_part, 0, unroll=8)
    pack(0, antennas)
    for tile in range(tiles):
        polyphase(frames, w_ref, tile, 8, first // 8 - 1, taps, store_rest)

    between()

    @pl.when(t > 0)
    def _():
        landing = joined.at[:, pl.ds(0, halo)]
        pltpu.make_async_copy(landing, landing, halo_sems.at[1]).wait()

    for tile in range(tiles):
        polyphase(frames, w_ref, tile, 0, 1, taps, store_rest)

    def rest_part(i, _):
        starts = [(h * eighth + i * 2 + p) * rest_stride for p in range(2) for h in range(4)]
        y = dft(gather(early, starts, first))
        for p in range(2):
            cols = slice(p * LANES, (p + 1) * LANES)
            re, im = y[:channels, cols], y[channels:, cols]
            row = antennas + i * 2 + p
            turn(row, jnp.where(quarter, re, pltpu.roll(im, LANES // 4, 1)))
            turn(row + eighth, jnp.where(quarter, pltpu.roll(re, LANES - LANES // 4, 1), im))
        return 0

    lax.fori_loop(0, eighth // 2, rest_part, 0, unroll=4)
    pack(antennas, paired)


def correlate_kernel(
    tms,
    groups,
    scale,
    v_ref,
    window_ref,
    table_ref,
    r_ref,
    joined,
    w_ref,
    c_ref,
    early,
    late,
    turned,
    s_ref,
    x_ref,
    right,
    left,
    outs,
    ready,
    load_sems,
    halo_sems,
    send1,
    recv1,
    send2,
    recv2,
    send3,
    recv3,
):
    t, f = lax.axis_index("tm"), lax.axis_index("freq")
    g, k = f // 2, f % 2
    half = tms // 2
    peers = tms * groups
    rows = s_ref.shape[1]
    ants = 2 * rows // 3
    sibling = (t, 2 * g + 1 - k)
    mine = g // 2 % half
    my_high = g // (2 * half)

    halo = joined.shape[1] - v_ref.shape[1]
    loads = [
        pltpu.make_async_copy(source, target, load_sems.at[i])
        for i, (source, target) in enumerate(
            (
                (v_ref, joined.at[:, pl.ds(halo, v_ref.shape[1])]),
                (window_ref, w_ref),
                (table_ref, c_ref),
            )
        )
    ]
    for load in loads:
        load.start()
    barrier = pltpu.get_barrier_semaphore()

    def greet(to):
        pl.semaphore_signal(barrier, inc=1, device_id=to, device_id_type=MESH)

    column = [(lax.rem(t + i, tms), 2 * g + k) for i in range(1, tms)]
    for i in range(1, groups):
        greet((t, 2 * lax.rem(g + i, groups) + k))
    for to in column + [sibling] + [(half * k + j, 2 * g + 1 - k) for j in range(half)]:
        greet(to)
    pl.semaphore_wait(barrier, groups + tms - 1 + jnp.where(k == t // half, 0, tms))
    for to in column:
        pl.semaphore_signal(ready, inc=1, device_id=to, device_id_type=MESH)

    last = v_ref.at[:, pl.ds(v_ref.shape[1] - halo, halo)]
    landing = joined.at[:, pl.ds(0, halo)]

    @pl.when(t < tms - 1)
    def _():
        pltpu.make_async_remote_copy(
            src_ref=last,
            dst_ref=landing,
            send_sem=halo_sems.at[0],
            recv_sem=halo_sems.at[1],
            device_id=(lax.rem(t + 1, tms), f),
            device_id_type=MESH,
        ).start()

    def send_phase(n, first_row, row_count):
        def send_block(i, _):
            tt = lax.rem(t + tms + (1 - 2 * k) * (i // 2), tms)
            part = lax.rem(mine + 2 * half - tt % half - n // 2, half)
            high = lax.rem(my_high + tt // half + n % 2, 2)
            gg = (high * half + part) * 2 + lax.rem(g + i, 2)
            some = pl.ds(first_row, row_count)
            src = s_ref.at[gg * tms + tt, some]
            dst = x_ref.at[k, mine, my_high, g % 2, t, some]
            here = (tt == t) & (gg == g)

            @pl.when(here)
            def _():
                pltpu.make_async_copy(src, dst, recv1.at[n]).start()

            @pl.when(jnp.logical_not(here))
            def _():
                pltpu.make_async_remote_copy(
                    src_ref=src,
                    dst_ref=dst,
                    send_sem=send1,
                    recv_sem=recv1.at[n],
                    device_id=(tt, 2 * gg + k),
                    device_id_type=MESH,
                ).start()

            return 0

        lax.fori_loop(0, 2 * tms, send_block, 0)
        return 0

    def send_phases(first, last, first_row, row_count):
        lax.fori_loop(first, last, lambda n, _: send_phase(n, first_row, row_count), 0)

    def send_early():
        pl.semaphore_wait(ready, tms - 1)
        send_phases(0, EARLY, 0, ants)

    channelize(
        v_ref,
        w_ref,
        c_ref,
        s_ref,
        joined,
        early,
        late,
        turned,
        loads,
        halo_sems,
        t,
        send_early,
    )
    send_phases(0, EARLY, ants, rows - ants)
    send_phases(EARLY, tms, 0, rows)

    wide = tms * LANES
    lane = lax.broadcasted_iota(jnp.int32, (ants, LANES), 1)
    low = lane < LANES // 2
    quarter = lane % (LANES // 2) < LANES // 4
    block = ants * 4
    own = block // 2
    slot = t % half
    dims = (((1,), (1,)), ((), ()))

    def place(n):
        return lax.rem(my_high + t // half + n % 2, 2), lax.rem(mine + t + n // 2, half)

    def phase(n, _):
        high, part = place(n)
        arrived = x_ref.at[k, part, high]
        pltpu.make_async_copy(arrived, arrived, recv1.at[n]).wait()
        pltpu.make_async_remote_copy(
            src_ref=arrived,
            dst_ref=arrived,
            send_sem=send3,
            recv_sem=recv3.at[n],
            device_id=sibling,
            device_id_type=MESH,
        ).start()

        def assemble(kk, mine_too):
            for low_g in range(2):
                base = pl.multiple_of((2 * low_g + kk) * ants, ants)

                def put(at, cols, value, turned_value):
                    count = value.shape[0]
                    right[n, pl.ds(base + at, count), cols] = value
                    if mine_too:
                        left[n, 0, low_g * ants + at : low_g * ants + at + count, cols] = value
                        left[n, 1, low_g * ants + at : low_g * ants + at + count, cols] = (
                            turned_value(value)
                        )

                def turn_wide(v):
                    v = pltpu.roll(v, LANES // 2, 1)
                    return jnp.where(low[: v.shape[0]], v, -v)

                def turn_narrow(v):
                    ahead = pltpu.roll(v, LANES - LANES // 4, 1)
                    behind = pltpu.roll(v, LANES // 4, 1)
                    return jnp.where(quarter[: v.shape[0]], ahead, -behind)

                for tt in range(tms):
                    cols = slice(tt * LANES, (tt + 1) * LANES)
                    put(0, cols, x_ref[kk, part, high, low_g, tt, :ants, :], turn_wide)
                for tt in range(0, tms, 2):
                    h0 = x_ref[kk, part, high, low_g, tt, ants:, :]
                    h1 = x_ref[kk, part, high, low_g, tt + 1, ants:, :]
                    some = low[: ants // 2]
                    cols = slice(wide + tt // 2 * LANES, wide + (tt // 2 + 1) * LANES)
                    top = jnp.where(some, h0, pltpu.roll(h1, LANES // 2, 1))
                    put(0, cols, top, turn_narrow)
                    bottom = jnp.where(some, pltpu.roll(h0, LANES // 2, 1), h1)
                    put(ants // 2, cols, bottom, turn_narrow)

        assemble(k, True)

        def piece(row, row_count, col, col_count):
            value = lax.dot_general(
                left[pl.ds(row, row_count)].reshape(row_count * block, -1),
                right[pl.ds(col, col_count)].reshape(col_count * block, -1),
                dims,
                preferred_element_type=jnp.float32,
            )
            value = (value * scale).astype(jnp.bfloat16)
            value = value.reshape(row_count, 2, 2, ants, col_count * block)
            for r in range(row_count):
                to_high, to_part = place(row + r)
                target = to_high * half + to_part
                here = (t == target) & (k == t // half)
                for c in range(col_count):
                    at_high, at_part = place(col + c)
                    cols = pl.ds(pl.multiple_of((at_high * half + at_part) * block, block), block)
                    outs[row + r, :, :, :, cols] = value[r, :, :, :, c * block : (c + 1) * block]
                    src = outs.at[row + r, :, :, :, cols]
                    dst = r_ref.at[:, slot, :, k, :, cols]

                    @pl.when(here)
                    def _():
                        pltpu.make_async_copy(src, dst, recv2).start()

                    @pl.when(jnp.logical_not(here))
                    def _():
                        pltpu.make_async_remote_copy(
                            src_ref=src,
                            dst_ref=dst,
                            send_sem=send2,
                            recv_sem=recv2,
                            device_id=(target, 2 * g + t // half),
                            device_id_type=MESH,
                        ).start()

        def row_pair(i, _):
            piece(n, 1, 2 * i, 2)
            return 0

        def column_pair(i, _):
            piece(2 * i, 2, n, 1)
            return 0

        lax.fori_loop(0, n // 2, row_pair, 0)

        @pl.when(n % 2 == 1)
        def _():
            piece(n, 1, n - 1, 1)

        other = x_ref.at[1 - k, part, high]
        pltpu.make_async_copy(other, other, recv3.at[n]).wait()
        assemble(1 - k, False)
        lax.fori_loop(0, (n + 1) // 2, column_pair, 0)

        @pl.when(n % 2 == 0)
        def _():
            piece(n, 1, n, 1)

        return 0

    lax.fori_loop(0, tms, phase, 0)
    pltpu.make_async_copy(r_ref, r_ref, recv2).wait()

    @pl.when(t < tms - 1)
    def _():
        pltpu.make_async_copy(landing, landing, halo_sems.at[0]).wait()

    pltpu.make_async_copy(x_ref.at[k], x_ref.at[k], send3).wait()
    sent = s_ref.at[pl.ds(0, peers - 1)]
    pltpu.make_async_copy(sent, sent, send1).wait()

    @pl.when(k == t // half)
    def _():
        kept = outs.at[pl.ds(0, tms - 1)]
        pltpu.make_async_copy(kept, kept, send2).wait()

    @pl.when(k != t // half)
    def _():
        pltpu.make_async_copy(outs, outs, send2).wait()


def cast_kernel(pieces, r_ref, o_ref, taken, wide, read_sems, write_sems):
    rows = r_ref.shape[0] // pieces
    slices = [pl.ds(i * rows, rows) for i in range(pieces)]
    reads = [
        pltpu.make_async_copy(r_ref.at[some], taken.at[some], read_sems.at[i])
        for i, some in enumerate(slices)
    ]
    writes = [
        pltpu.make_async_copy(wide.at[some], o_ref.at[some], write_sems.at[i])
        for i, some in enumerate(slices)
    ]
    for read in reads:
        read.start()
    for some, read, write in zip(slices, reads, writes):
        read.wait()
        wide[some] = taken[some].astype(jnp.float32)
        write.start()
    for write in writes:
        write.wait()


def cast(values):
    pieces = 8
    anywhere = pl.BlockSpec(memory_space=pl.ANY)
    return pl.pallas_call(
        functools.partial(cast_kernel, pieces),
        out_shape=jax.ShapeDtypeStruct(values.shape, jnp.float32),
        in_specs=[anywhere],
        out_specs=anywhere,
        scratch_shapes=[
            pltpu.VMEM(values.shape, jnp.bfloat16),
            pltpu.VMEM(values.shape, jnp.float32),
            pltpu.SemaphoreType.DMA((pieces,)),
            pltpu.SemaphoreType.DMA((pieces,)),
        ],
        compiler_params=pltpu.CompilerParams(vmem_limit_bytes=60 << 20),
    )(values)


def local(voltages, window):
    tms, freqs = lax.axis_size("tm"), lax.axis_size("freq")
    groups = freqs // 2
    half = tms // 2
    taps, period = window.shape
    antennas, samples = voltages.shape
    spec_here = samples // period
    channels = period // 2
    assert channels == tms * groups
    rows = antennas * 3 // 2
    total = antennas * freqs
    row_count = total // tms
    depth = 2 * spec_here * tms
    result = pl.pallas_call(
        functools.partial(correlate_kernel, tms, groups, (spec_here * tms) ** (-0.5)),
        out_shape=jax.ShapeDtypeStruct((2, half, 2, 2, antennas, total), jnp.bfloat16),
        in_specs=[pl.BlockSpec(memory_space=pl.ANY)] * 3,
        out_specs=pl.BlockSpec(memory_space=pl.ANY),
        scratch_shapes=[
            pltpu.VMEM((antennas, samples + (taps - 1) * period), jnp.bfloat16),
            pltpu.VMEM(window.shape, jnp.float32),
            pltpu.VMEM((4 * channels, period), jnp.bfloat16),
            pltpu.VMEM((period // LANES, antennas * (spec_here // 3 + 1), LANES), jnp.float32),
            pltpu.VMEM((period // LANES, antennas * (2 * spec_here // 3 + 1), LANES), jnp.float32),
            pltpu.VMEM((channels * (rows + 1), LANES), jnp.float32),
            pltpu.VMEM((channels, rows, LANES), jnp.bfloat16),
            pltpu.VMEM((2, half, 2, 2, tms, rows, LANES), jnp.bfloat16),
            pltpu.VMEM((tms, row_count, depth), jnp.bfloat16),
            pltpu.VMEM((tms, 2, row_count // 2, depth), jnp.bfloat16),
            pltpu.VMEM((tms, 2, 2, antennas, total), jnp.bfloat16),
            pltpu.SemaphoreType.REGULAR,
            pltpu.SemaphoreType.DMA((3,)),
            pltpu.SemaphoreType.DMA((2,)),
            pltpu.SemaphoreType.DMA,
            pltpu.SemaphoreType.DMA((tms,)),
            pltpu.SemaphoreType.DMA,
            pltpu.SemaphoreType.DMA,
            pltpu.SemaphoreType.DMA,
            pltpu.SemaphoreType.DMA((tms,)),
        ],
        compiler_params=pltpu.CompilerParams(
            collective_id=0, has_side_effects=True, vmem_limit_bytes=60 << 20
        ),
        cost_estimate=pl.CostEstimate(
            flops=2 * 2 * (total // 2) * total * depth, bytes_accessed=8 << 20, transcendentals=0
        ),
    )(voltages, window, jnp.asarray(dft_table(period, channels)))
    return cast(result.reshape(2 * half * row_count, total)).reshape(2, half, row_count, total)


def solution(mesh):
    return jax.shard_map(
        local,
        mesh=mesh,
        in_specs=(P("freq", "tm"), P()),
        out_specs=P(None, "freq", "tm", None),
        check_vma=False,
    )
```

```python
import functools
import math

import jax
import jax.numpy as jnp
import numpy as np
from jax import lax
from jax.experimental import pallas as pl
from jax.experimental.pallas import tpu as pltpu
from jax.sharding import PartitionSpec as P

MESH = pl.DeviceIdType.MESH
LANES = 128
EARLY = 1


def dft_table(length, channels):
    sample, channel = np.arange(length), np.arange(channels)
    phase = (channel[:, None] * sample[None, :] % length) * (2.0 * math.pi / length)
    rows = np.concatenate([np.cos(phase), -np.sin(phase)], axis=0) * length ** (-0.5)
    high = rows.astype(jnp.bfloat16)
    low = (rows - high.astype(np.float64)).astype(jnp.bfloat16)
    return np.concatenate([high, low], axis=0)


def polyphase(frames, w_ref, tile, first, groups, taps, store):
    cols = slice(tile * LANES, (tile + 1) * LANES)
    weights = [w_ref[k : k + 1, cols] for k in range(taps)]

    def group(i, held):
        held = list(held)
        for u in range(8):
            at = first + i * 8 + u
            held.append(frames(at + taps - 1, tile))
            value = weights[0] * held[0]
            for k in range(1, taps):
                value = value + weights[k] * held[k]
            held.pop(0)
            store(at, tile, value)
        return tuple(held)

    lax.fori_loop(0, groups, group, tuple(frames(first + j, tile) for j in range(taps - 1)))


def channelize(
    v_ref, w_ref, c_ref, s_ref, joined, early, late, turned, loads, halo_sems, t, between
):
    taps, period = w_ref.shape
    antennas, samples = v_ref.shape
    spec = samples // period
    first, main = spec // 3, 2 * spec // 3
    tiles = period // LANES
    channels = period // 2
    halo = (taps - 1) * period
    paired = antennas // 2
    eighth = antennas // 4
    main_stride, rest_stride = main + 1, first + 1
    turn_stride = s_ref.shape[1] + 1

    def frames(j, tile):
        at = pl.multiple_of(j * period + tile * LANES, LANES)
        return joined[:, pl.ds(at, LANES)].astype(jnp.float32)

    def store_main(at, tile, value):
        for h in range(2):
            rows = pl.ds(h * paired * main_stride + at - first, paired, stride=main_stride)
            late[tile, rows, :] = value[h * paired : (h + 1) * paired]

    def store_rest(at, tile, value):
        for h in range(4):
            rows = pl.ds(h * eighth * rest_stride + at, eighth, stride=rest_stride)
            early[tile, rows, :] = value[h * eighth : (h + 1) * eighth]

    @pl.when(t == 0)
    def _():
        joined[:, :halo] = jnp.zeros((antennas, halo), jnp.bfloat16)

    window_load, middle, last, table, begin = loads
    window_load.wait()
    middle.wait()
    for tile in range(tiles):
        polyphase(frames, w_ref, tile, first, first // 8, taps, store_main)
    last.wait()
    for tile in range(tiles):
        polyphase(frames, w_ref, tile, 2 * first, first // 8, taps, store_main)
    table.wait()

    lane = lax.broadcasted_iota(jnp.int32, (channels, LANES), 1)
    low = lane < LANES // 2
    quarter = lane % (LANES // 2) < LANES // 4
    dims = (((1,), (1,)), ((), ()))

    def dft(x):
        high = x.astype(jnp.bfloat16)
        rest = (x - high.astype(jnp.float32)).astype(jnp.bfloat16)
        y = lax.dot_general(c_ref[...], high, dims, preferred_element_type=jnp.float32)
        z = lax.dot_general(
            c_ref[: 2 * channels, :], rest, dims, preferred_element_type=jnp.float32
        )
        return y[: 2 * channels] + y[2 * channels :] + z

    def gather(ref, starts, count):
        return jnp.concatenate(
            [
                jnp.concatenate([ref[tile, pl.ds(at, count), :] for at in starts], axis=0)
                for tile in range(tiles)
            ],
            axis=1,
        )

    def turn(row, value):
        turned[pl.ds(row, channels, stride=turn_stride), :] = value

    def pack(at, count):
        def some(i, _):
            for u in range(16):
                c = i * 16 + u
                s_ref[c, pl.ds(at, count), :] = turned[
                    pl.ds(c * turn_stride + at, count), :
                ].astype(jnp.bfloat16)
            return 0

        lax.fori_loop(0, channels // 16, some, 0)

    def main_part(i, _):
        starts = [(h * paired + i * 2 + p) * main_stride for p in range(2) for h in range(2)]
        y = dft(gather(late, starts, main))
        for p in range(2):
            cols = slice(p * LANES, (p + 1) * LANES)
            re, im = y[:channels, cols], y[channels:, cols]
            turn(i * 2 + p, jnp.where(low, re, pltpu.roll(im, LANES // 2, 1)))
            turn(i * 2 + p + paired, jnp.where(low, pltpu.roll(re, LANES // 2, 1), im))
        return 0

    lax.fori_loop(0, paired // 2, main_part, 0, unroll=8)
    pack(0, antennas)
    begin.wait()
    for tile in range(tiles):
        polyphase(frames, w_ref, tile, 8, first // 8 - 1, taps, store_rest)

    between()

    @pl.when(t > 0)
    def _():
        landing = joined.at[:, pl.ds(0, halo)]
        pltpu.make_async_copy(landing, landing, halo_sems.at[1]).wait()

    for tile in range(tiles):
        polyphase(frames, w_ref, tile, 0, 1, taps, store_rest)

    def rest_part(i, _):
        starts = [(h * eighth + i * 2 + p) * rest_stride for p in range(2) for h in range(4)]
        y = dft(gather(early, starts, first))
        for p in range(2):
            cols = slice(p * LANES, (p + 1) * LANES)
            re, im = y[:channels, cols], y[channels:, cols]
            row = antennas + i * 2 + p
            turn(row, jnp.where(quarter, re, pltpu.roll(im, LANES // 4, 1)))
            turn(row + eighth, jnp.where(quarter, pltpu.roll(re, LANES - LANES // 4, 1), im))
        return 0

    lax.fori_loop(0, eighth // 2, rest_part, 0, unroll=4)
    pack(antennas, paired)


def correlate_kernel(
    tms,
    groups,
    scale,
    v_ref,
    window_ref,
    table_ref,
    r_ref,
    joined,
    w_ref,
    c_ref,
    early,
    late,
    turned,
    s_ref,
    x_ref,
    right,
    left,
    outs,
    ready,
    load_sems,
    halo_sems,
    send1,
    recv1,
    send2,
    recv2,
    send3,
    recv3,
):
    t, f = lax.axis_index("tm"), lax.axis_index("freq")
    g, k = f // 2, f % 2
    half = tms // 2
    peers = tms * groups
    rows = s_ref.shape[1]
    ants = 2 * rows // 3
    sibling = (t, 2 * g + 1 - k)
    mine = g // 2 % half
    my_high = g // (2 * half)

    halo = joined.shape[1] - v_ref.shape[1]
    third = v_ref.shape[1] // 3
    moves = [(window_ref, w_ref)]
    for start, stop in ((third - halo, 2 * third), (2 * third, 3 * third), (0, third - halo)):
        target = joined.at[:, pl.ds(halo + start, stop - start)]
        moves.append((v_ref.at[:, pl.ds(start, stop - start)], target))
    moves.insert(3, (table_ref, c_ref))
    loads = [
        pltpu.make_async_copy(source, target, load_sems.at[i])
        for i, (source, target) in enumerate(moves)
    ]
    for load in loads:
        load.start()
    barrier = pltpu.get_barrier_semaphore()

    def greet(to):
        pl.semaphore_signal(barrier, inc=1, device_id=to, device_id_type=MESH)

    column = [(lax.rem(t + i, tms), 2 * g + k) for i in range(1, tms)]
    for i in range(1, groups):
        greet((t, 2 * lax.rem(g + i, groups) + k))
    for to in column + [sibling] + [(half * k + j, 2 * g + 1 - k) for j in range(half)]:
        greet(to)
    pl.semaphore_wait(barrier, groups + tms - 1 + jnp.where(k == t // half, 0, tms))
    for to in column:
        pl.semaphore_signal(ready, inc=1, device_id=to, device_id_type=MESH)

    last = v_ref.at[:, pl.ds(v_ref.shape[1] - halo, halo)]
    landing = joined.at[:, pl.ds(0, halo)]

    @pl.when(t < tms - 1)
    def _():
        pltpu.make_async_remote_copy(
            src_ref=last,
            dst_ref=landing,
            send_sem=halo_sems.at[0],
            recv_sem=halo_sems.at[1],
            device_id=(lax.rem(t + 1, tms), f),
            device_id_type=MESH,
        ).start()

    def send_phase(n, first_row, row_count):
        def send_block(i, _):
            tt = lax.rem(t + i // 2, tms)
            part = lax.rem(mine + 2 * half - tt % half - n // 2, half)
            high = lax.rem(my_high + tt // half + n % 2, 2)
            gg = (high * half + part) * 2 + lax.rem(g + i, 2)
            some = pl.ds(first_row, row_count)
            src = s_ref.at[gg * tms + tt, some]
            dst = x_ref.at[k, mine, my_high, g % 2, t, some]
            here = (tt == t) & (gg == g)

            @pl.when(here)
            def _():
                pltpu.make_async_copy(src, dst, recv1.at[n]).start()

            @pl.when(jnp.logical_not(here))
            def _():
                pltpu.make_async_remote_copy(
                    src_ref=src,
                    dst_ref=dst,
                    send_sem=send1,
                    recv_sem=recv1.at[n],
                    device_id=(tt, 2 * gg + k),
                    device_id_type=MESH,
                ).start()

            return 0

        lax.fori_loop(0, 2 * tms, send_block, 0)
        return 0

    def send_phases(first, last, first_row, row_count):
        lax.fori_loop(first, last, lambda n, _: send_phase(n, first_row, row_count), 0)

    def send_early():
        pl.semaphore_wait(ready, tms - 1)
        send_phases(0, EARLY, 0, ants)

    channelize(
        v_ref,
        w_ref,
        c_ref,
        s_ref,
        joined,
        early,
        late,
        turned,
        loads,
        halo_sems,
        t,
        send_early,
    )
    send_phases(0, EARLY, ants, rows - ants)
    send_phases(EARLY, tms, 0, rows)

    wide = tms * LANES
    lane = lax.broadcasted_iota(jnp.int32, (ants, LANES), 1)
    low = lane < LANES // 2
    quarter = lane % (LANES // 2) < LANES // 4
    block = ants * 4
    own = block // 2
    slot = t % half
    dims = (((1,), (1,)), ((), ()))

    def place(n):
        return lax.rem(my_high + t // half + n % 2, 2), lax.rem(mine + t + n // 2, half)

    def phase(n, _):
        high, part = place(n)
        arrived = x_ref.at[k, part, high]
        pltpu.make_async_copy(arrived, arrived, recv1.at[n]).wait()
        pltpu.make_async_remote_copy(
            src_ref=arrived,
            dst_ref=arrived,
            send_sem=send3,
            recv_sem=recv3.at[n],
            device_id=sibling,
            device_id_type=MESH,
        ).start()

        def assemble(kk, mine_too):
            for low_g in range(2):
                base = pl.multiple_of((2 * low_g + kk) * ants, ants)

                def put(at, cols, value, turned_value):
                    count = value.shape[0]
                    right[n, pl.ds(base + at, count), cols] = value
                    if mine_too:
                        left[n, 0, low_g * ants + at : low_g * ants + at + count, cols] = value
                        left[n, 1, low_g * ants + at : low_g * ants + at + count, cols] = (
                            turned_value(value)
                        )

                def turn_wide(v):
                    v = pltpu.roll(v, LANES // 2, 1)
                    return jnp.where(low[: v.shape[0]], v, -v)

                def turn_narrow(v):
                    ahead = pltpu.roll(v, LANES - LANES // 4, 1)
                    behind = pltpu.roll(v, LANES // 4, 1)
                    return jnp.where(quarter[: v.shape[0]], ahead, -behind)

                for tt in range(tms):
                    cols = slice(tt * LANES, (tt + 1) * LANES)
                    put(0, cols, x_ref[kk, part, high, low_g, tt, :ants, :], turn_wide)
                for tt in range(0, tms, 2):
                    h0 = x_ref[kk, part, high, low_g, tt, ants:, :]
                    h1 = x_ref[kk, part, high, low_g, tt + 1, ants:, :]
                    some = low[: ants // 2]
                    cols = slice(wide + tt // 2 * LANES, wide + (tt // 2 + 1) * LANES)
                    top = jnp.where(some, h0, pltpu.roll(h1, LANES // 2, 1))
                    put(0, cols, top, turn_narrow)
                    bottom = jnp.where(some, pltpu.roll(h0, LANES // 2, 1), h1)
                    put(ants // 2, cols, bottom, turn_narrow)

        assemble(k, True)

        def piece(row, row_count, col, col_count):
            value = lax.dot_general(
                left[pl.ds(row, row_count)].reshape(row_count * block, -1),
                right[pl.ds(col, col_count)].reshape(col_count * block, -1),
                dims,
                preferred_element_type=jnp.float32,
            )
            value = (value * scale).astype(jnp.bfloat16)
            value = value.reshape(row_count, 2, 2, ants, col_count * block)
            for r in range(row_count):
                to_high, to_part = place(row + r)
                target = to_high * half + to_part
                here = (t == target) & (k == t // half)
                for c in range(col_count):
                    at_high, at_part = place(col + c)
                    cols = pl.ds(pl.multiple_of((at_high * half + at_part) * block, block), block)
                    outs[row + r, :, :, :, cols] = value[r, :, :, :, c * block : (c + 1) * block]
                    src = outs.at[row + r, :, :, :, cols]
                    dst = r_ref.at[:, slot, :, k, :, cols]

                    @pl.when(here)
                    def _():
                        pltpu.make_async_copy(src, dst, recv2).start()

                    @pl.when(jnp.logical_not(here))
                    def _():
                        pltpu.make_async_remote_copy(
                            src_ref=src,
                            dst_ref=dst,
                            send_sem=send2,
                            recv_sem=recv2,
                            device_id=(target, 2 * g + t // half),
                            device_id_type=MESH,
                        ).start()

        def row_pair(i, _):
            piece(n, 1, 2 * i, 2)
            return 0

        def column_pair(i, _):
            piece(2 * i, 2, n, 1)
            return 0

        lax.fori_loop(0, n // 2, row_pair, 0)

        @pl.when(n % 2 == 1)
        def _():
            piece(n, 1, n - 1, 1)

        other = x_ref.at[1 - k, part, high]
        pltpu.make_async_copy(other, other, recv3.at[n]).wait()
        assemble(1 - k, False)
        lax.fori_loop(0, (n + 1) // 2, column_pair, 0)

        @pl.when(n % 2 == 0)
        def _():
            piece(n, 1, n, 1)

        return 0

    lax.fori_loop(0, tms, phase, 0)
    pltpu.make_async_copy(r_ref, r_ref, recv2).wait()

    @pl.when(t < tms - 1)
    def _():
        pltpu.make_async_copy(landing, landing, halo_sems.at[0]).wait()

    pltpu.make_async_copy(x_ref.at[k], x_ref.at[k], send3).wait()
    sent = s_ref.at[pl.ds(0, peers - 1)]
    pltpu.make_async_copy(sent, sent, send1).wait()

    @pl.when(k == t // half)
    def _():
        kept = outs.at[pl.ds(0, tms - 1)]
        pltpu.make_async_copy(kept, kept, send2).wait()

    @pl.when(k != t // half)
    def _():
        pltpu.make_async_copy(outs, outs, send2).wait()


def cast_kernel(pieces, r_ref, o_ref, taken, wide, read_sems, write_sems):
    rows = r_ref.shape[0] // pieces
    slices = [pl.ds(i * rows, rows) for i in range(pieces)]
    reads = [
        pltpu.make_async_copy(r_ref.at[some], taken.at[some], read_sems.at[i])
        for i, some in enumerate(slices)
    ]
    writes = [
        pltpu.make_async_copy(wide.at[some], o_ref.at[some], write_sems.at[i])
        for i, some in enumerate(slices)
    ]
    for read in reads:
        read.start()
    for some, read, write in zip(slices, reads, writes):
        read.wait()
        wide[some] = taken[some].astype(jnp.float32)
        write.start()
    for write in writes:
        write.wait()


def cast(values):
    pieces = 8
    anywhere = pl.BlockSpec(memory_space=pl.ANY)
    return pl.pallas_call(
        functools.partial(cast_kernel, pieces),
        out_shape=jax.ShapeDtypeStruct(values.shape, jnp.float32),
        in_specs=[anywhere],
        out_specs=anywhere,
        scratch_shapes=[
            pltpu.VMEM(values.shape, jnp.bfloat16),
            pltpu.VMEM(values.shape, jnp.float32),
            pltpu.SemaphoreType.DMA((pieces,)),
            pltpu.SemaphoreType.DMA((pieces,)),
        ],
        compiler_params=pltpu.CompilerParams(vmem_limit_bytes=60 << 20),
    )(values)


def local(voltages, window):
    tms, freqs = lax.axis_size("tm"), lax.axis_size("freq")
    groups = freqs // 2
    half = tms // 2
    taps, period = window.shape
    antennas, samples = voltages.shape
    spec_here = samples // period
    channels = period // 2
    assert channels == tms * groups
    rows = antennas * 3 // 2
    total = antennas * freqs
    row_count = total // tms
    depth = 2 * spec_here * tms
    result = pl.pallas_call(
        functools.partial(correlate_kernel, tms, groups, (spec_here * tms) ** (-0.5)),
        out_shape=jax.ShapeDtypeStruct((2, half, 2, 2, antennas, total), jnp.bfloat16),
        in_specs=[pl.BlockSpec(memory_space=pl.ANY)] * 3,
        out_specs=pl.BlockSpec(memory_space=pl.ANY),
        scratch_shapes=[
            pltpu.VMEM((antennas, samples + (taps - 1) * period), jnp.bfloat16),
            pltpu.VMEM(window.shape, jnp.float32),
            pltpu.VMEM((4 * channels, period), jnp.bfloat16),
            pltpu.VMEM((period // LANES, antennas * (spec_here // 3 + 1), LANES), jnp.float32),
            pltpu.VMEM((period // LANES, antennas * (2 * spec_here // 3 + 1), LANES), jnp.float32),
            pltpu.VMEM((channels * (rows + 1), LANES), jnp.float32),
            pltpu.VMEM((channels, rows, LANES), jnp.bfloat16),
            pltpu.VMEM((2, half, 2, 2, tms, rows, LANES), jnp.bfloat16),
            pltpu.VMEM((tms, row_count, depth), jnp.bfloat16),
            pltpu.VMEM((tms, 2, row_count // 2, depth), jnp.bfloat16),
            pltpu.VMEM((tms, 2, 2, antennas, total), jnp.bfloat16),
            pltpu.SemaphoreType.REGULAR,
            pltpu.SemaphoreType.DMA((5,)),
            pltpu.SemaphoreType.DMA((2,)),
            pltpu.SemaphoreType.DMA,
            pltpu.SemaphoreType.DMA((tms,)),
            pltpu.SemaphoreType.DMA,
            pltpu.SemaphoreType.DMA,
            pltpu.SemaphoreType.DMA,
            pltpu.SemaphoreType.DMA((tms,)),
        ],
        compiler_params=pltpu.CompilerParams(
            collective_id=0, has_side_effects=True, vmem_limit_bytes=60 << 20
        ),
        cost_estimate=pl.CostEstimate(
            flops=2 * 2 * (total // 2) * total * depth, bytes_accessed=8 << 20, transcendentals=0
        ),
    )(voltages, window, jnp.asarray(dft_table(period, channels)))
    return cast(result.reshape(2 * half * row_count, total)).reshape(2, half, row_count, total)


def solution(mesh):
    return jax.shard_map(
        local,
        mesh=mesh,
        in_specs=(P("freq", "tm"), P()),
        out_specs=P(None, "freq", "tm", None),
        check_vma=False,
    )
```
